512 devices in a mesh: section: 16 (over y, x), tensor: 32 (over z, core).
Axes of the slice: x: 4, y: 4, z: 16, core: 2. Of those that a mesh axis runs over, the one named last changes fastest.
Arguments:
- section_inputs: bfloat16 [16, 2, 128, 8192], P('section', None, None, 'tensor'), may hold values from -6 to 6
- out_grad: bfloat16 [2, 128, 8192], P(None, None, 'tensor'), may hold values from -6 to 6
- w1: bfloat16 [16, 64, 128, 128], P('section', 'tensor'), may hold values from -0.5 to 0.5
- w2: bfloat16 [16, 64, 128, 512], P('section', 'tensor'), may hold values from -0.5 to 0.5
- w3: bfloat16 [16, 64, 512, 128], P('section', 'tensor'), may hold values from -0.25 to 0.25
- w4: bfloat16 [16, 64, 128, 128], P('section', 'tensor'), may hold values from -0.25 to 0.25
Outputs:
- grad_inputs: bfloat16 [16, 2, 128, 8192], P('section', None, None, 'tensor')
- grad_w1: float32 [16, 64, 128, 128], P('section', 'tensor')
- grad_w2: float32 [16, 64, 128, 512], P('section', 'tensor')
- grad_w3: float32 [16, 64, 512, 128], P('section', 'tensor')
- grad_w4: float32 [16, 64, 128, 128], P('section', 'tensor')
The draws below stay inside these ranges and needn't reach their ends.
All inputs are finite; a program needn't handle non-finite values.
Results may differ from the reference program's by a relative error of at most 0.035.
Values may be sent and summed in bfloat16 or wider, within the bound.
No kernel may reach another device: no remote copies, remote signals or barrier semaphores. Data moves between devices by JAX's collectives and lax.ppermute only.
A program may use at most 64 MiB of HBM per device.

```python
import jax
import jax.numpy as jnp
from jax import lax

D = 8192
MONARCH_BLOCKS = 64
TOK = 128
MB = 2
MONARCH_WIDTH = 128
HB = 512
SECTIONS = 16


def steps_of(key, extent, shards, smallest, top_value):
    level = 1.0
    for dim, blocks in shards:
        draws = jax.random.uniform(jax.random.fold_in(jax.random.fold_in(key, 6), dim), (blocks,), jnp.float32, smallest / len(shards), top_value / len(shards))
        level = level * jnp.repeat(jnp.exp(draws), extent[dim] // blocks).reshape((-1,) + (1,) * (len(extent) - 1 - dim))
    return level


def normal_values(own_key, shape, scale, limit, cuts=(), held_as=jnp.bfloat16):
    result = jax.random.normal(own_key, shape, jnp.float32) * scale
    if len(cuts) > 0:
        result = steps_of(own_key, shape, cuts, -0.22, 0.18) * result
    return jnp.clip(result, min=-limit, max=limit).astype(held_as)


def setup_inputs(seed: int = 0) -> dict:
    keys = jax.random.split(jax.random.key(seed), 7)
    section_inputs = normal_values(keys[0], (SECTIONS, MB, TOK, D), 1.0, 6.0, ((0, 16), (3, 32)))
    out_grad = normal_values(keys[1], (MB, TOK, D), 1.0, 6.0, ((2, 32),))
    w1 = normal_values(keys[2], (SECTIONS, MONARCH_BLOCKS, MONARCH_WIDTH, MONARCH_WIDTH), MONARCH_WIDTH ** -0.5, 0.5, ((0, 16), (1, 32)))
    w2 = normal_values(keys[3], (SECTIONS, MONARCH_BLOCKS, MONARCH_WIDTH, HB), MONARCH_WIDTH ** -0.5, 0.5, ((0, 16), (1, 32)))
    w3 = normal_values(keys[4], (SECTIONS, MONARCH_BLOCKS, HB, MONARCH_WIDTH), HB ** -0.5, 0.25, ((0, 16), (1, 32)))
    w4 = normal_values(keys[5], (SECTIONS, MONARCH_BLOCKS, MONARCH_WIDTH, MONARCH_WIDTH), (4 * MONARCH_WIDTH) ** -0.5, 0.25, ((0, 16), (1, 32)))
    return {"section_inputs": section_inputs, "out_grad": out_grad, "w1": w1, "w2": w2, "w3": w3, "w4": w4}


SQRT_TWO_PI = 0.7978845608028654
CUBIC_TERM = 0.044715


def gelu_tanh(linear):
    inner = SQRT_TWO_PI * (linear + CUBIC_TERM * linear * linear * linear)
    return 0.5 * linear * (1.0 + jnp.tanh(inner))


def gelu_slope(linear):
    inner = SQRT_TWO_PI * (linear + CUBIC_TERM * linear * linear * linear)
    tangent = jnp.tanh(inner)
    return 0.5 * (1.0 + tangent) + 0.5 * linear * (1.0 - tangent * tangent) * SQRT_TWO_PI * (1.0 + 3.0 * CUBIC_TERM * linear * linear)


def mixing_rows(form, left_side, right_side):
    return jnp.einsum(form, left_side.astype(jnp.float32), right_side.astype(jnp.float32), precision=lax.Precision.HIGHEST)


def reference(section_inputs, out_grad, w1, w2, w3, w4):
    all_rows = MB * TOK
    spread_rows = MONARCH_WIDTH // MONARCH_BLOCKS
    outgoing_gradient = out_grad.reshape(all_rows, MONARCH_BLOCKS, MONARCH_WIDTH)
    inputs_list = []
    leading_weights = []
    second_list = []
    third_list = []
    closing_weights = []
    for section_id in range(SECTIONS - 1, -1, -1):
        input_rows = section_inputs[section_id].reshape(all_rows, MONARCH_BLOCKS, MONARCH_WIDTH)
        leading_weight = w1[section_id]
        w_second = w2[section_id].reshape(MONARCH_BLOCKS, MONARCH_BLOCKS, spread_rows, HB)
        w_third = w3[section_id]
        closing_weight = w4[section_id].reshape(MONARCH_BLOCKS, MONARCH_BLOCKS, spread_rows, MONARCH_WIDTH)
        raised_rows = mixing_rows('owz,wzy->wyo', input_rows, leading_weight).astype(jnp.bfloat16)
        mixed_in = raised_rows.reshape(MONARCH_BLOCKS, MONARCH_BLOCKS, spread_rows, all_rows)
        linear = mixing_rows('abrt,barn->bnt', mixed_in, w_second)
        gelu_out = gelu_tanh(linear).astype(jnp.bfloat16)
        lowered = mixing_rows('bnt,bnk->bkt', gelu_out, w_third).astype(jnp.bfloat16)
        handed_back = lowered.reshape(MONARCH_BLOCKS, MONARCH_BLOCKS, spread_rows, all_rows)
        lower_gradient = mixing_rows('zqs,qhis->hqiz', outgoing_gradient, closing_weight).astype(jnp.bfloat16)
        grad_mid = lower_gradient.reshape(MONARCH_BLOCKS, MONARCH_WIDTH, all_rows)
        grad_hid = mixing_rows('bkt,bnk->bnt', grad_mid, w_third)
        grad_lin = (grad_hid * gelu_slope(linear)).astype(jnp.bfloat16)
        grad_up = mixing_rows('bnt,barn->abrt', grad_lin, w_second).astype(jnp.bfloat16)
        gradient_returned = grad_up.reshape(MONARCH_BLOCKS, MONARCH_WIDTH, all_rows)
        incoming_gradient = (outgoing_gradient.astype(jnp.float32) + mixing_rows('vip,vwi->pvw', gradient_returned, leading_weight)).astype(jnp.bfloat16)
        closing_weights.append(mixing_rows('nxpq,qxf->xnpf', handed_back, outgoing_gradient).reshape(MONARCH_BLOCKS, MONARCH_WIDTH, MONARCH_WIDTH))
        third_list.append(mixing_rows('bnt,bkt->bnk', gelu_out, grad_mid))
        second_list.append(mixing_rows('abrt,bnt->barn', mixed_in, grad_lin).reshape(MONARCH_BLOCKS, MONARCH_WIDTH, HB))
        leading_weights.append(mixing_rows('qln,lvq->lnv', input_rows, gradient_returned))
        inputs_list.append(incoming_gradient.reshape(MB, TOK, D))
        outgoing_gradient = incoming_gradient
    grad_inputs = jnp.stack(inputs_list[::-1])
    grad_w1 = jnp.stack(leading_weights[::-1])
    grad_w2 = jnp.stack(second_list[::-1])
    grad_w3 = jnp.stack(third_list[::-1])
    grad_w4 = jnp.stack(closing_weights[::-1])
    return (grad_inputs, grad_w1, grad_w2, grad_w3, grad_w4)
```

```python
import jax
import jax.numpy as jnp
from jax import lax
from jax.experimental import pallas as pl
from jax.experimental.pallas import tpu as pltpu
from jax.sharding import PartitionSpec as P

SQRT_TWO_PI = 0.7978845608028654
CUBIC_TERM = 0.044715
MIB = 2**20

IN_VMEM = pl.BlockSpec(memory_space=pltpu.VMEM)
IN_SMEM = pl.BlockSpec(memory_space=pltpu.SMEM)
IN_PLACE = pl.BlockSpec(memory_space=pl.ANY)


def gelu_tanh(linear):
    inner = SQRT_TWO_PI * (linear + CUBIC_TERM * linear * linear * linear)
    return 0.5 * linear * (1.0 + jnp.tanh(inner))


def gelu_slope(linear):
    inner = SQRT_TWO_PI * (linear + CUBIC_TERM * linear * linear * linear)
    tangent = jnp.tanh(inner)
    return 0.5 * (1.0 + tangent) + 0.5 * linear * (1.0 - tangent * tangent) * SQRT_TWO_PI * (
        1.0 + 3.0 * CUBIC_TERM * linear * linear
    )


def matrix_product(form, left_side, right_side):
    return jnp.einsum(form, left_side, right_side, preferred_element_type=jnp.float32)


def exchange_blocks(source, target, blocks, rows):
    for row in range(rows):
        turned = source[pl.ds(row, blocks, stride=rows), :].T
        target[pl.ds(row, blocks, stride=rows), :] = jnp.concatenate(
            [turned[:blocks], turned[blocks:]], axis=1
        )


def load_second_body(gathered, second, sems):
    copy = pltpu.make_async_copy(gathered, second, sems.at[0])
    copy.start()
    copy.wait()


def load_rest_body(gathered, fourth, third, first, sems):
    hidden = third.shape[3]
    width = third.shape[2]
    copies = []
    for half in range(2):
        copies.append((gathered.at[:, pl.ds(half * width, width), :], fourth.at[:, half]))
    base = 2 * width
    for half in range(2):
        for part in range(hidden // width):
            start = base + half * hidden + part * width
            copies.append(
                (
                    gathered.at[:, pl.ds(start, width), :],
                    third.at[:, half, :, pl.ds(part * width, width)],
                )
            )
    base = base + 2 * hidden
    for half in range(2):
        copies.append((gathered.at[:, pl.ds(base + half * width, width), :], first.at[:, half]))
    started = [
        pltpu.make_async_copy(source, target, sems.at[number])
        for number, (source, target) in enumerate(copies)
    ]
    for copy in started:
        copy.start()
    for copy in started:
        copy.wait()


def slope_body(raised, second, slope, rows_in, rows_out):
    blocks, rows, width = raised.shape
    rows_in[...] = raised[...].astype(jnp.float32).reshape(blocks * rows, width)
    exchange_blocks(rows_in, rows_out, blocks, rows)
    for b in range(blocks):
        mixed = rows_out[pl.ds(b * rows, rows), :].astype(jnp.bfloat16)
        linear = lax.dot_general(
            mixed,
            second[b // 2, b % 2],
            (((1,), (1,)), ((), ())),
            preferred_element_type=jnp.float32,
        )
        slope[b] = gelu_slope(linear)


def section_body(
    active,
    cotangent,
    old_cotangent,
    old_gv,
    old_gu,
    slope,
    fourth,
    third,
    second,
    first,
    result,
    kept_cotangent,
    kept_gv,
    kept_gu,
    rows_in,
    rows_out,
    grad_lin,
):
    blocks, rows, width = cotangent.shape

    @pl.when(active[0] == 0)
    def _():
        result[...] = cotangent[...]
        kept_cotangent[...] = old_cotangent[...]
        kept_gv[...] = old_gv[...]
        kept_gu[...] = old_gu[...]

    @pl.when(active[0] != 0)
    def _():
        kept_cotangent[...] = cotangent[...]
        for a in range(blocks):
            rows_in[pl.ds(a * rows, rows), :] = jnp.dot(
                cotangent[a], fourth[a // 2, a % 2], preferred_element_type=jnp.float32
            )
        exchange_blocks(rows_in, rows_out, blocks, rows)
        kept_gv[...] = rows_out[...].reshape(blocks, rows, width).astype(jnp.bfloat16)
        for b in range(blocks):
            grad_hid = jnp.dot(
                kept_gv[b], third[b // 2, b % 2], preferred_element_type=jnp.float32
            )
            grad_lin[b] = (grad_hid * slope[b]).astype(jnp.bfloat16)
        for b in range(blocks):
            rows_in[pl.ds(b * rows, rows), :] = jnp.dot(
                grad_lin[b], second[b // 2, b % 2], preferred_element_type=jnp.float32
            )
        exchange_blocks(rows_in, rows_out, blocks, rows)
        kept_gu[...] = rows_out[...].reshape(blocks, rows, width).astype(jnp.bfloat16)
        for a in range(blocks):
            term = jnp.dot(kept_gu[a], first[a // 2, a % 2], preferred_element_type=jnp.float32)
            result[a] = (cotangent[a].astype(jnp.float32) + term).astype(jnp.bfloat16)


def load_second(gathered, devices, hidden, width):
    return pl.pallas_call(
        load_second_body,
        out_shape=pltpu.VMEM((devices, 2, hidden, width), jnp.bfloat16),
        in_specs=[IN_PLACE],
        out_specs=IN_VMEM,
        scratch_shapes=[pltpu.SemaphoreType.DMA((1,))],
        compiler_params=pltpu.CompilerParams(vmem_limit_bytes=16 * MIB),
        name="load_second",
    )(gathered)


def load_rest(gathered, devices, hidden, width):
    return pl.pallas_call(
        load_rest_body,
        out_shape=[
            pltpu.VMEM((devices, 2, width, width), jnp.bfloat16),
            pltpu.VMEM((devices, 2, width, hidden), jnp.bfloat16),
            pltpu.VMEM((devices, 2, width, width), jnp.bfloat16),
        ],
        in_specs=[IN_PLACE],
        out_specs=[IN_VMEM] * 3,
        scratch_shapes=[pltpu.SemaphoreType.DMA((4 + 2 * (hidden // width),))],
        compiler_params=pltpu.CompilerParams(vmem_limit_bytes=24 * MIB),
        name="load_rest",
    )(gathered)


def row_slopes(raised, second):
    blocks, rows, width = raised.shape
    hidden = second.shape[2]
    return pl.pallas_call(
        slope_body,
        out_shape=jax.ShapeDtypeStruct((blocks, rows, hidden), jnp.float32),
        in_specs=[IN_VMEM] * 2,
        out_specs=IN_VMEM,
        scratch_shapes=[pltpu.VMEM((blocks * rows, width), jnp.float32)] * 2,
        compiler_params=pltpu.CompilerParams(vmem_limit_bytes=12 * MIB),
        name="row_slopes",
    )(raised, second)


def section_step(active, cotangent, kept, slope, weights):
    blocks, rows, width = cotangent.shape
    hidden = slope.shape[2]
    return pl.pallas_call(
        section_body,
        out_shape=[jax.ShapeDtypeStruct(cotangent.shape, jnp.bfloat16)] * 4,
        in_specs=[IN_SMEM] + [IN_VMEM] * 9,
        out_specs=[IN_VMEM] * 4,
        scratch_shapes=[pltpu.VMEM((blocks * rows, width), jnp.float32)] * 2
        + [pltpu.VMEM((blocks, rows, hidden), jnp.bfloat16)],
        compiler_params=pltpu.CompilerParams(vmem_limit_bytes=12 * MIB),
        name="section_step",
    )(active, cotangent, *kept, slope, *weights)


def to_owners(value):
    return lax.all_to_all(value, "tensor", split_axis=0, concat_axis=0, tiled=True)


def local(section_inputs, out_grad, w1, w2, w3, w4):
    devices = lax.axis_size("tensor")
    section_count = lax.axis_size("section")
    section_id = lax.axis_index("section")
    all_rows = section_inputs.shape[1] * section_inputs.shape[2]
    owned = w1.shape[1]
    width = w1.shape[2]
    hidden = w2.shape[3]
    blocks = owned * devices
    spread = width // blocks
    rows = all_rows // devices
    parts = hidden // width

    natural = lax.broadcasted_iota(jnp.int32, (width, width), 0)
    grouped = lax.broadcasted_iota(jnp.int32, (width, width), 1)
    reorder = (grouped == (natural % spread) * blocks + natural // spread).astype(jnp.bfloat16)

    second_local = matrix_product("bkn,kp->bnp", w2[0], reorder).astype(jnp.bfloat16)
    fourth_local = matrix_product("akc,kp->acp", w4[0], reorder).astype(jnp.bfloat16)
    third_local = matrix_product(
        "bqnk,kp->bqpn", w3[0].reshape(owned, parts, width, width), reorder
    ).astype(jnp.bfloat16)
    first_local = matrix_product("ack,kp->apc", w1[0], reorder).astype(jnp.bfloat16)
    rest_local = jnp.concatenate(
        [
            fourth_local.reshape(owned * width, width),
            third_local.reshape(owned * hidden, width),
            first_local.reshape(owned * width, width),
        ],
        axis=0,
    )
    second_all = lax.all_gather(second_local, "tensor", axis=0, tiled=False)
    rest_all = lax.all_gather(rest_local, "tensor", axis=0, tiled=False)

    input_rows = section_inputs[0].reshape(all_rows, owned, width)
    raised_rows = matrix_product("owz,wzy->wyo", input_rows, w1[0]).astype(jnp.bfloat16)
    raised_grouped = matrix_product("tac,apc->atp", input_rows, first_local).astype(jnp.bfloat16)
    raised_grouped = raised_grouped.reshape(owned, devices, rows, width).transpose(1, 0, 2, 3)
    targets = out_grad.reshape(devices, rows, owned, width).transpose(0, 2, 1, 3)
    by_rows = to_owners(jnp.concatenate([raised_grouped, targets], axis=2))
    by_rows = by_rows.reshape(blocks, 2 * rows, width)
    raised_here = by_rows[:, :rows]
    cotangent = by_rows[:, rows:]

    mixed = lax.all_to_all(raised_rows, "tensor", split_axis=1, concat_axis=0, tiled=True)
    mixed = mixed.reshape(blocks, owned, spread, all_rows)
    linear = matrix_product("abrt,barn->btn", mixed, w2[0].reshape(owned, blocks, spread, hidden))
    gelu_out = gelu_tanh(linear).astype(jnp.bfloat16)
    slope_owned = gelu_slope(linear)
    lowered = matrix_product("btn,bnk->bkt", gelu_out, w3[0]).astype(jnp.bfloat16)
    handed_back = lax.all_to_all(lowered, "tensor", split_axis=1, concat_axis=0, tiled=True)
    handed_back = handed_back.reshape(blocks, owned, spread, all_rows)

    second = load_second(second_all, devices, hidden, width)
    slope = row_slopes(raised_here, second)
    fourth, third, first = load_rest(rest_all, devices, hidden, width)
    weights = (fourth, third, second, first)
    kept = (cotangent, cotangent, cotangent)
    for step in range(section_count):
        turn = section_count - 1 - step
        active = (section_id == turn).astype(jnp.int32).reshape(1)
        cotangent, *kept = section_step(active, cotangent, kept, slope, weights)
        if turn > 0:
            cotangent = lax.ppermute(cotangent, "section", [(turn, turn - 1)])

    sent = jnp.concatenate(kept, axis=1).reshape(devices, owned, 3, rows, width)
    returned = to_owners(sent)
    returned = returned.transpose(2, 1, 0, 3, 4).reshape(3, owned, all_rows, width)
    gy, gv, gu = returned[0], returned[1], returned[2]
    grad_inputs = gy.astype(jnp.float32) + matrix_product("atp,apc->atc", gu, first_local)
    grad_inputs = grad_inputs.astype(jnp.bfloat16).transpose(1, 0, 2)
    grad_hid = matrix_product("btp,bqpn->btqn", gv, third_local).reshape(owned, all_rows, hidden)
    grad_lin = (grad_hid * slope_owned).astype(jnp.bfloat16)
    gv = matrix_product("btp,kp->btk", gv, reorder).astype(jnp.bfloat16)
    gu = matrix_product("atp,kp->atk", gu, reorder).astype(jnp.bfloat16)
    grad_w1 = matrix_product("tac,atk->ack", input_rows, gu)
    grad_w2 = matrix_product("abrt,btn->barn", mixed, grad_lin).reshape(owned, width, hidden)
    grad_w3 = matrix_product("btn,btk->bnk", gelu_out, gv)
    grad_w4 = matrix_product("nxpq,xqf->xnpf", handed_back, gy).reshape(owned, width, width)
    grad_inputs = grad_inputs.reshape(section_inputs.shape)
    return (grad_inputs, grad_w1[None], grad_w2[None], grad_w3[None], grad_w4[None])


def solution(mesh):
    in_specs = (
        P("section", None, None, "tensor"),
        P(None, None, "tensor"),
        P("section", "tensor", None, None),
        P("section", "tensor", None, None),
        P("section", "tensor", None, None),
        P("section", "tensor", None, None),
    )
    out_specs = (
        P("section", None, None, "tensor"),
        P("section", "tensor", None, None),
        P("section", "tensor", None, None),
        P("section", "tensor", None, None),
        P("section", "tensor", None, None),
    )
    return jax.shard_map(local, mesh=mesh, in_specs=in_specs, out_specs=out_specs, check_vma=False)
```

```python
import functools

import jax
import jax.numpy as jnp
from jax import lax
from jax.experimental import pallas as pl
from jax.experimental.pallas import tpu as pltpu
from jax.sharding import PartitionSpec as P

SQRT_TWO_PI = 0.7978845608028654
CUBIC_TERM = 0.044715
MIB = 2**20

IN_VMEM = pl.BlockSpec(memory_space=pltpu.VMEM)
IN_SMEM = pl.BlockSpec(memory_space=pltpu.SMEM)
IN_PLACE = pl.BlockSpec(memory_space=pl.ANY)


def gelu_tanh(linear):
    inner = SQRT_TWO_PI * (linear + CUBIC_TERM * linear * linear * linear)
    return 0.5 * linear * (1.0 + jnp.tanh(inner))


def gelu_slope(linear):
    inner = SQRT_TWO_PI * (linear + CUBIC_TERM * linear * linear * linear)
    tangent = jnp.tanh(inner)
    return 0.5 * (1.0 + tangent) + 0.5 * linear * (1.0 - tangent * tangent) * SQRT_TWO_PI * (
        1.0 + 3.0 * CUBIC_TERM * linear * linear
    )


def matrix_product(form, left_side, right_side):
    return jnp.einsum(form, left_side, right_side, preferred_element_type=jnp.float32)


def exchange_blocks(source, target, blocks, rows):
    for row in range(rows):
        turned = source[pl.ds(row, blocks, stride=rows), :].T
        target[pl.ds(row, blocks, stride=rows), :] = jnp.concatenate(
            [turned[:blocks], turned[blocks:]], axis=1
        )


def contract_last(left_side, right_side):
    return lax.dot_general(
        left_side, right_side, (((1,), (1,)), ((), ())), preferred_element_type=jnp.float32
    )


def order_matrix(width, blocks, spread):
    grouped = lax.broadcasted_iota(jnp.int32, (width, width), 0)
    natural = lax.broadcasted_iota(jnp.int32, (width, width), 1)
    here = grouped == (natural % spread) * blocks + natural // spread
    return jnp.where(here, 1.0, 0.0).astype(jnp.bfloat16)


def prepare_body(blocks, w1, w2, w3, w4, packed):
    owned, width, hidden = w2.shape
    order = order_matrix(width, blocks, width // blocks)
    base = 0
    for b in range(owned):
        turned = jnp.dot(order, w2[b], preferred_element_type=jnp.float32).T
        packed[pl.ds(base, hidden), :] = turned.astype(jnp.bfloat16)
        base += hidden
    for a in range(owned):
        turned = jnp.dot(order, w4[a], preferred_element_type=jnp.float32).T
        packed[pl.ds(base, width), :] = turned.astype(jnp.bfloat16)
        base += width
    for b in range(owned):
        for part in range(hidden // width):
            piece = contract_last(order, w3[b, pl.ds(part * width, width), :])
            packed[pl.ds(base, width), :] = piece.astype(jnp.bfloat16)
            base += width
    for a in range(owned):
        packed[pl.ds(base, width), :] = contract_last(order, w1[a]).astype(jnp.bfloat16)
        base += width


def start_loading(gathered, second, fourth, third, first, sems):
    owned, width, hidden = third.shape[1:]
    groups = []
    base = 0
    for target, length in ((second, hidden), (fourth, width)):
        group = []
        for half in range(owned):
            group.append((gathered.at[:, pl.ds(base, length), :], target.at[:, half]))
            base += length
        groups.append(group)
    group = []
    for half in range(owned):
        for part in range(hidden // width):
            place = third.at[:, half, :, pl.ds(part * width, width)]
            group.append((gathered.at[:, pl.ds(base, width), :], place))
            base += width
    groups.append(group)
    group = []
    for half in range(owned):
        group.append((gathered.at[:, pl.ds(base, width), :], first.at[:, half]))
        base += width
    groups.append(group)
    started = []
    number = 0
    for group in groups:
        copies = []
        for source, target in group:
            copy = pltpu.make_async_copy(source, target, sems.at[number])
            copy.start()
            copies.append(copy)
            number += 1
        started.append(copies)
    return started


def wait_all(copies):
    for copy in copies:
        copy.wait()


def first_body(
    turn,
    section,
    by_rows,
    gathered,
    result,
    kept,
    slope,
    second,
    fourth,
    third,
    first,
    rows_in,
    rows_out,
    grad_lin,
    sems,
):
    blocks, _, rows, width = by_rows.shape
    owned = third.shape[1]
    to_second, to_fourth, to_third, to_first = start_loading(
        gathered, second, fourth, third, first, sems
    )
    rows_in[...] = by_rows[:, 0].astype(jnp.float32).reshape(blocks * rows, width)
    exchange_blocks(rows_in, rows_out, blocks, rows)
    wait_all(to_second)
    for b in range(blocks):
        mixed = rows_out[pl.ds(b * rows, rows), :].astype(jnp.bfloat16)
        slope[b] = gelu_slope(contract_last(mixed, second[b // owned, b % owned]))
    wait_all(to_fourth)
    wait_all(to_third)
    wait_all(to_first)

    @pl.when(section[0] != turn)
    def _():
        result[...] = by_rows[:, 1]
        for kind in range(kept.shape[1]):
            kept[:, kind] = by_rows[:, 1]

    @pl.when(section[0] == turn)
    def _():
        result[...] = by_rows[:, 1]
        one_section(
            result, kept, slope, second, fourth, third, first, rows_in, rows_out, grad_lin
        )


def one_section(result, kept, slope, second, fourth, third, first, rows_in, rows_out, grad_lin):
    blocks, rows, width = result.shape
    owned = third.shape[1]
    kept[:, 0] = result[...]
    for a in range(blocks):
        rows_in[pl.ds(a * rows, rows), :] = jnp.dot(
            kept[a, 0], fourth[a // owned, a % owned], preferred_element_type=jnp.float32
        )
    exchange_blocks(rows_in, rows_out, blocks, rows)
    kept[:, 1] = rows_out[...].reshape(blocks, rows, width).astype(jnp.bfloat16)
    for b in range(blocks):
        grad_hid = jnp.dot(
            kept[b, 1], third[b // owned, b % owned], preferred_element_type=jnp.float32
        )
        grad_lin[b] = (grad_hid * slope[b]).astype(jnp.bfloat16)
    for b in range(blocks):
        rows_in[pl.ds(b * rows, rows), :] = jnp.dot(
            grad_lin[b], second[b // owned, b % owned], preferred_element_type=jnp.float32
        )
    exchange_blocks(rows_in, rows_out, blocks, rows)
    kept[:, 2] = rows_out[...].reshape(blocks, rows, width).astype(jnp.bfloat16)
    for a in range(blocks):
        term = jnp.dot(
            kept[a, 2], first[a // owned, a % owned], preferred_element_type=jnp.float32
        )
        result[a] = (kept[a, 0].astype(jnp.float32) + term).astype(jnp.bfloat16)


def step_body(
    turn,
    section,
    cotangent,
    old_kept,
    slope,
    second,
    fourth,
    third,
    first,
    result,
    kept,
    rows_in,
    rows_out,
    grad_lin,
):
    result[...] = cotangent[...]

    @pl.when(section[0] != turn)
    def _():
        kept[...] = old_kept[...]

    @pl.when(section[0] == turn)
    def _():
        one_section(
            result, kept, slope, second, fourth, third, first, rows_in, rows_out, grad_lin
        )


def reload_body(gathered, second, fourth, third, first, sems):
    for copies in start_loading(gathered, second, fourth, third, first, sems):
        wait_all(copies)


def gradients_body(
    returned,
    w1,
    w3,
    inputs,
    mixed,
    gelu_rows,
    slope,
    handed_back,
    grad_inputs,
    grad_w1,
    grad_w2,
    grad_w3,
    grad_w4,
):
    devices, owned, _, rows, width = returned.shape
    order = order_matrix(width, devices * owned, width // (devices * owned))

    def rows_of(block, kind):
        value = returned[:, block, kind].astype(jnp.float32)
        return value.reshape(devices * rows, width)

    def in_natural_order(value):
        return jnp.dot(
            value.astype(jnp.bfloat16), order, preferred_element_type=jnp.float32
        ).astype(jnp.bfloat16)

    for a in range(owned):
        gy = rows_of(a, 0)
        gu = in_natural_order(rows_of(a, 2))
        grad_inputs[:, a * width : (a + 1) * width] = (gy + contract_last(gu, w1[a])).astype(
            jnp.bfloat16
        )
        grad_w1[a] = jnp.dot(inputs[a], gu, preferred_element_type=jnp.float32)
        grad_w4[a] = jnp.dot(
            handed_back[a], gy.astype(jnp.bfloat16), preferred_element_type=jnp.float32
        )
    for b in range(owned):
        gv = in_natural_order(rows_of(b, 1))
        grad_lin = (contract_last(w3[b], gv) * slope[b]).astype(jnp.bfloat16)
        grad_w2[b] = contract_last(mixed[b], grad_lin)
        grad_w3[b] = jnp.dot(gelu_rows[b], gv, preferred_element_type=jnp.float32)


def in_vmem(count):
    return [IN_VMEM] * count


def to_owners(value):
    return lax.all_to_all(value, "tensor", split_axis=0, concat_axis=0, tiled=True)


def tied(value, anchor):
    return lax.optimization_barrier((value, anchor))[0]


def local(section_inputs, out_grad, w1, w2, w3, w4):
    devices = lax.axis_size("tensor")
    section_count = lax.axis_size("section")
    section = lax.axis_index("section").astype(jnp.int32).reshape(1)
    all_rows = section_inputs.shape[1] * section_inputs.shape[2]
    owned, width, hidden = w2.shape[1:]
    blocks = owned * devices
    spread = width // blocks
    rows = all_rows // devices
    packed_rows = owned * (2 * hidden + 2 * width)
    bf16, f32 = jnp.bfloat16, jnp.float32

    packed = pl.pallas_call(
        functools.partial(prepare_body, blocks),
        out_shape=jax.ShapeDtypeStruct((packed_rows, width), bf16),
        in_specs=in_vmem(4),
        out_specs=IN_VMEM,
        compiler_params=pltpu.CompilerParams(vmem_limit_bytes=16 * MIB),
        name="prepare_weights",
    )(w1[0], w2[0], w3[0], w4[0])
    gathered = lax.all_gather(packed, "tensor", axis=0, tiled=False)

    input_rows = section_inputs[0].reshape(all_rows, owned, width)
    first_local = packed[packed_rows - owned * width :].reshape(owned, width, width)
    raised = matrix_product("tac,apc->atp", input_rows, first_local).astype(bf16)
    raised = raised.reshape(owned, devices, rows, width).transpose(1, 0, 2, 3)
    targets = out_grad.reshape(devices, rows, owned, width).transpose(0, 2, 1, 3)
    by_rows = to_owners(jnp.stack([raised, targets], axis=2))
    by_rows = by_rows.reshape(blocks, 2, rows, width)

    def forward(input_rows, w1, w2, w3):
        raised_rows = matrix_product("owz,wzy->wyo", input_rows, w1).astype(bf16)
        mixed = lax.all_to_all(raised_rows, "tensor", split_axis=1, concat_axis=0, tiled=True)
        mixed = mixed.reshape(blocks, owned, spread, all_rows).transpose(1, 0, 2, 3)
        mixed = mixed.reshape(owned, width, all_rows)
        linear = matrix_product("bkt,bkn->bnt", mixed, w2)
        gelu_rows = gelu_tanh(linear).astype(bf16)
        slope = gelu_slope(linear)
        lowered = matrix_product("bnt,bnk->bkt", gelu_rows, w3).astype(bf16)
        back = lax.all_to_all(lowered, "tensor", split_axis=1, concat_axis=0, tiled=True)
        back = back.reshape(blocks, owned, spread, all_rows).transpose(1, 0, 2, 3)
        back = back.reshape(owned, width, all_rows)
        return input_rows.transpose(1, 2, 0), mixed, gelu_rows, slope, back

    weight_shapes = [
        pltpu.VMEM((devices, owned, hidden, width), bf16),
        pltpu.VMEM((devices, owned, width, width), bf16),
        pltpu.VMEM((devices, owned, width, hidden), bf16),
        pltpu.VMEM((devices, owned, width, width), bf16),
    ]
    copies = pltpu.SemaphoreType.DMA((owned * (3 + hidden // width),))
    row_shape = jax.ShapeDtypeStruct((blocks, rows, width), bf16)
    kept_shape = jax.ShapeDtypeStruct((blocks, 3, rows, width), bf16)
    scratch = [
        pltpu.VMEM((blocks * rows, width), f32),
        pltpu.VMEM((blocks * rows, width), f32),
        pltpu.VMEM((blocks, rows, hidden), bf16),
    ]
    last = section_count - 1
    cotangent, kept, slope, *weights = pl.pallas_call(
        functools.partial(first_body, last),
        out_shape=[row_shape, kept_shape, pltpu.VMEM((blocks, rows, hidden), f32)]
        + weight_shapes,
        in_specs=[IN_SMEM, IN_VMEM, IN_PLACE],
        out_specs=in_vmem(7),
        scratch_shapes=scratch + [copies],
        compiler_params=pltpu.CompilerParams(vmem_limit_bytes=36 * MIB),
        name="load_and_first_section",
    )(section, by_rows, gathered)
    forward_values = None
    for turn in range(last, -1, -1):
        if turn < last:
            cotangent = lax.ppermute(cotangent, "section", [(turn + 1, turn)])
            cotangent, kept = pl.pallas_call(
                functools.partial(step_body, turn),
                out_shape=[row_shape, kept_shape],
                in_specs=[IN_SMEM] + in_vmem(7),
                out_specs=in_vmem(2),
                scratch_shapes=scratch,
                compiler_params=pltpu.CompilerParams(vmem_limit_bytes=8 * MIB),
                name="section_step",
            )(section, cotangent, kept, slope, *weights)
        if turn == section_count // 2:
            given = tied((input_rows, w1[0], w2[0], w3[0]), kept)
            forward_values = forward(*given)
            gathered = tied(gathered, forward_values)
            weights = pl.pallas_call(
                reload_body,
                out_shape=weight_shapes,
                in_specs=[IN_PLACE],
                out_specs=in_vmem(4),
                scratch_shapes=[copies],
                compiler_params=pltpu.CompilerParams(vmem_limit_bytes=36 * MIB),
                name="load_again",
            )(gathered)

    returned = to_owners(kept.reshape(devices, owned, 3, rows, width))
    grad_inputs, *grads = pl.pallas_call(
        gradients_body,
        out_shape=[
            jax.ShapeDtypeStruct((all_rows, owned * width), bf16),
            jax.ShapeDtypeStruct((owned, width, width), f32),
            jax.ShapeDtypeStruct((owned, width, hidden), f32),
            jax.ShapeDtypeStruct((owned, hidden, width), f32),
            jax.ShapeDtypeStruct((owned, width, width), f32),
        ],
        in_specs=in_vmem(8),
        out_specs=in_vmem(5),
        compiler_params=pltpu.CompilerParams(vmem_limit_bytes=24 * MIB),
        name="gradients",
    )(returned, w1[0], w3[0], *forward_values)
    grad_inputs = grad_inputs.reshape(section_inputs.shape)
    return (grad_inputs, *[grad[None] for grad in grads])


def solution(mesh):
    in_specs = (
        P("section", None, None, "tensor"),
        P(None, None, "tensor"),
        P("section", "tensor", None, None),
        P("section", "tensor", None, None),
        P("section", "tensor", None, None),
        P("section", "tensor", None, None),
    )
    out_specs = (
        P("section", None, None, "tensor"),
        P("section", "tensor", None, None),
        P("section", "tensor", None, None),
        P("section", "tensor", None, None),
        P("section", "tensor", None, None),
    )
    return jax.shard_map(local, mesh=mesh, in_specs=in_specs, out_specs=out_specs, check_vma=False)
```

```python
import functools

import jax
import jax.numpy as jnp
from jax import lax
from jax.experimental import pallas as pl
from jax.experimental.pallas import tpu as pltpu
from jax.sharding import PartitionSpec as P

SQRT_TWO_PI = 0.7978845608028654
CUBIC_TERM = 0.044715
MIB = 2**20

IN_VMEM = pl.BlockSpec(memory_space=pltpu.VMEM)
IN_SMEM = pl.BlockSpec(memory_space=pltpu.SMEM)
IN_HBM = pl.BlockSpec(memory_space=pltpu.HBM)


def gelu_tanh(linear):
    inner = SQRT_TWO_PI * (linear + CUBIC_TERM * linear * linear * linear)
    return 0.5 * linear * (1.0 + jnp.tanh(inner))


def gelu_slope(linear):
    inner = SQRT_TWO_PI * (linear + CUBIC_TERM * linear * linear * linear)
    tangent = jnp.tanh(inner)
    return 0.5 * (1.0 + tangent) + 0.5 * linear * (1.0 - tangent * tangent) * SQRT_TWO_PI * (
        1.0 + 3.0 * CUBIC_TERM * linear * linear
    )


def matrix_product(form, left_side, right_side):
    return jnp.einsum(form, left_side, right_side, preferred_element_type=jnp.float32)


def exchange_blocks(source, target, blocks, rows):
    for row in range(rows):
        turned = source[pl.ds(row, blocks, stride=rows), :].T
        target[pl.ds(row, blocks, stride=rows), :] = jnp.concatenate(
            [turned[:blocks], turned[blocks:]], axis=1
        )


def contract_last(left_side, right_side):
    return lax.dot_general(
        left_side, right_side, (((1,), (1,)), ((), ())), preferred_element_type=jnp.float32
    )


def order_matrix(width, blocks, spread):
    grouped = lax.broadcasted_iota(jnp.int32, (width, width), 0)
    natural = lax.broadcasted_iota(jnp.int32, (width, width), 1)
    here = grouped == (natural % spread) * blocks + natural // spread
    return jnp.where(here, 1.0, 0.0).astype(jnp.bfloat16)


def prepare_body(blocks, w1_far, w2_far, w3_far, w4_far, packed, w1, w2, w3, w4, sems):
    owned, width, hidden = w2.shape
    pairs = ((w2_far, w2), (w4_far, w4), (w3_far, w3), (w1_far, w1))
    copies = [pltpu.make_async_copy(*pair, sems.at[i]) for i, pair in enumerate(pairs)]
    for copy in copies:
        copy.start()
    order = order_matrix(width, blocks, width // blocks)
    for copy in copies:
        copy.wait()
    base = 0
    for b in range(owned):
        turned = jnp.dot(order, w2[b], preferred_element_type=jnp.float32).T
        packed[pl.ds(base, hidden), :] = turned.astype(jnp.bfloat16)
        base += hidden
    for a in range(owned):
        turned = jnp.dot(order, w4[a], preferred_element_type=jnp.float32).T
        packed[pl.ds(base, width), :] = turned.astype(jnp.bfloat16)
        base += width
    for b in range(owned):
        for part in range(hidden // width):
            piece = contract_last(order, w3[b, pl.ds(part * width, width), :])
            packed[pl.ds(base, width), :] = piece.astype(jnp.bfloat16)
            base += width
    for a in range(owned):
        packed[pl.ds(base, width), :] = contract_last(order, w1[a]).astype(jnp.bfloat16)
        base += width


def loads_of(gathered, paired, second, fourth, third, first, sems):
    owned, width, hidden = third.shape[1:]
    to_second, to_fourth, to_third, to_first = [], [], [], []
    base = 0
    for half in range(owned):
        to_second.append((gathered.at[:, pl.ds(base, hidden), :], second.at[:, half]))
        base += hidden
    for target, group, start in (
        (fourth, to_fourth, base),
        (first, to_first, base + owned * (width + hidden)),
    ):
        for half in range(owned):
            for side in range(2):
                piece = paired.at[:, side, pl.ds(start + half * width, width), :]
                place = target.at[:, pl.ds(half * width, width), pl.ds(side * width, width)]
                group.append((piece, place))
    base += owned * width
    for half in range(owned):
        for part in range(hidden // width):
            place = third.at[:, half, :, pl.ds(part * width, width)]
            to_third.append((gathered.at[:, pl.ds(base, width), :], place))
            base += width
    groups, number = [], 0
    for group in (to_second, to_fourth, to_third, to_first):
        copies = []
        for source, target in group:
            copies.append(pltpu.make_async_copy(source, target, sems.at[number]))
            number += 1
        groups.append(copies)
    return groups


def start_all(copies):
    for copy in copies:
        copy.start()


def block_tiles(rows_of, tiles):
    for number in range(tiles.shape[0]):
        four = [rows_of(4 * number + i) for i in range(4)]
        empty = jnp.zeros_like(four[0])
        spread = [
            jnp.concatenate([value, empty] if i % 2 == 0 else [empty, value], axis=1)
            for i, value in enumerate(four)
        ]
        product = jnp.dot(
            jnp.concatenate(spread, axis=0), tiles[number], preferred_element_type=jnp.float32
        )
        pair = 2 * four[0].shape[0]
        width = four[0].shape[1]
        yield 4 * number, product[:pair, :width]
        yield 4 * number + 2, product[pair:, width:]


def wait_all(copies):
    for copy in copies:
        copy.wait()


def first_body(
    turn,
    section,
    by_rows,
    gathered,
    paired,
    result,
    kept,
    slope,
    second,
    fourth,
    third,
    first,
    rows_in,
    rows_out,
    grad_lin,
    sems,
):
    blocks, _, rows, width = by_rows.shape
    owned = third.shape[1]
    to_second, to_fourth, to_third, to_first = loads_of(
        gathered, paired, second, fourth, third, first, sems
    )
    start_all(to_second + to_fourth)
    rows_in[...] = by_rows[:, 0].astype(jnp.float32).reshape(blocks * rows, width)
    exchange_blocks(rows_in, rows_out, blocks, rows)
    wait_all(to_second)
    start_all(to_third + to_first)
    for b in range(blocks):
        mixed = rows_out[pl.ds(b * rows, rows), :].astype(jnp.bfloat16)
        slope[b] = gelu_slope(contract_last(mixed, second[b // owned, b % owned]))

    @pl.when(section[0] != turn)
    def _():
        wait_all(to_fourth + to_third + to_first)
        result[...] = by_rows[:, 1]
        for kind in range(kept.shape[1]):
            kept[:, kind] = by_rows[:, 1]

    @pl.when(section[0] == turn)
    def _():
        result[...] = by_rows[:, 1]
        one_section(
            result,
            kept,
            slope,
            second,
            fourth,
            third,
            first,
            rows_in,
            rows_out,
            grad_lin,
            (to_fourth, to_third, to_first),
        )


def one_section(
    result,
    kept,
    slope,
    second,
    fourth,
    third,
    first,
    rows_in,
    rows_out,
    grad_lin,
    loads=((), (), ()),
):
    blocks, rows, width = result.shape
    owned = third.shape[1]
    kept[:, 0] = result[...]
    wait_all(loads[0])
    for a, product in block_tiles(lambda a: kept[a, 0], fourth):
        rows_in[pl.ds(a * rows, 2 * rows), :] = product
    exchange_blocks(rows_in, rows_out, blocks, rows)
    kept[:, 1] = rows_out[...].reshape(blocks, rows, width).astype(jnp.bfloat16)
    wait_all(loads[1])
    for b in range(blocks):
        grad_hid = jnp.dot(
            kept[b, 1], third[b // owned, b % owned], preferred_element_type=jnp.float32
        )
        grad_lin[b] = (grad_hid * slope[b]).astype(jnp.bfloat16)
    for b in range(blocks):
        rows_in[pl.ds(b * rows, rows), :] = jnp.dot(
            grad_lin[b], second[b // owned, b % owned], preferred_element_type=jnp.float32
        )
    exchange_blocks(rows_in, rows_out, blocks, rows)
    kept[:, 2] = rows_out[...].reshape(blocks, rows, width).astype(jnp.bfloat16)
    wait_all(loads[2])
    for a, product in block_tiles(lambda a: kept[a, 2], first):
        for i in range(2):
            total = kept[a + i, 0].astype(jnp.float32) + product[i * rows : (i + 1) * rows]
            result[a + i] = total.astype(jnp.bfloat16)


def step_body(
    turn,
    section,
    cotangent,
    old_kept,
    slope,
    second,
    fourth,
    third,
    first,
    result,
    kept,
    rows_in,
    rows_out,
    grad_lin,
):
    result[...] = cotangent[...]

    @pl.when(section[0] != turn)
    def _():
        kept[...] = old_kept[...]

    @pl.when(section[0] == turn)
    def _():
        one_section(
            result, kept, slope, second, fourth, third, first, rows_in, rows_out, grad_lin
        )


def gradients_body(
    returned,
    w1,
    w3,
    inputs,
    mixed,
    gelu_rows,
    slope,
    handed_back,
    grad_inputs,
    grad_w1,
    grad_w2,
    grad_w3,
    grad_w4,
):
    devices, owned, _, rows, width = returned.shape
    order = order_matrix(width, devices * owned, width // (devices * owned))

    def rows_of(block, kind):
        value = returned[:, block, kind].astype(jnp.float32)
        return value.reshape(devices * rows, width)

    def in_natural_order(value):
        return jnp.dot(
            value.astype(jnp.bfloat16), order, preferred_element_type=jnp.float32
        ).astype(jnp.bfloat16)

    for a in range(owned):
        gy = rows_of(a, 0)
        gu = in_natural_order(rows_of(a, 2))
        grad_inputs[:, a * width : (a + 1) * width] = (gy + contract_last(gu, w1[a])).astype(
            jnp.bfloat16
        )
        grad_w1[a] = jnp.dot(inputs[a], gu, preferred_element_type=jnp.float32)
        grad_w4[a] = jnp.dot(
            handed_back[a], gy.astype(jnp.bfloat16), preferred_element_type=jnp.float32
        )
    for b in range(owned):
        gv = in_natural_order(rows_of(b, 1))
        grad_lin = (contract_last(w3[b], gv) * slope[b]).astype(jnp.bfloat16)
        grad_w2[b] = contract_last(mixed[b], grad_lin)
        grad_w3[b] = jnp.dot(gelu_rows[b], gv, preferred_element_type=jnp.float32)


def in_vmem(count):
    return [IN_VMEM] * count


def to_owners(value):
    return lax.all_to_all(value, "tensor", split_axis=0, concat_axis=0, tiled=True)


def local(section_inputs, out_grad, w1, w2, w3, w4):
    devices = lax.axis_size("tensor")
    section_count = lax.axis_size("section")
    section = lax.axis_index("section").astype(jnp.int32).reshape(1)
    all_rows = section_inputs.shape[1] * section_inputs.shape[2]
    owned, width, hidden = w2.shape[1:]
    blocks = owned * devices
    spread = width // blocks
    rows = all_rows // devices
    packed_rows = owned * (2 * hidden + 2 * width)
    bf16, f32 = jnp.bfloat16, jnp.float32

    packed = pl.pallas_call(
        functools.partial(prepare_body, blocks),
        out_shape=jax.ShapeDtypeStruct((packed_rows, width), bf16),
        in_specs=[IN_HBM] * 4,
        out_specs=IN_VMEM,
        scratch_shapes=[pltpu.VMEM(w.shape[1:], bf16) for w in (w1, w2, w3, w4)]
        + [pltpu.SemaphoreType.DMA((4,))],
        compiler_params=pltpu.CompilerParams(vmem_limit_bytes=60 * MIB),
        name="prepare_weights",
    )(w1[0], w2[0], w3[0], w4[0])
    gathered = lax.all_gather(packed, "tensor", axis=0, tiled=False)

    input_rows = section_inputs[0].reshape(all_rows, owned, width)
    first_local = packed[packed_rows - owned * width :].reshape(owned, width, width)
    raised = matrix_product("tac,apc->atp", input_rows, first_local).astype(bf16)
    raised = raised.reshape(owned, devices, rows, width).transpose(1, 0, 2, 3)
    targets = out_grad.reshape(devices, rows, owned, width).transpose(0, 2, 1, 3)
    by_rows = to_owners(jnp.stack([raised, targets], axis=2))
    by_rows = by_rows.reshape(blocks, 2, rows, width)

    def forward(input_rows, w1, w2, w3):
        raised_rows = matrix_product("owz,wzy->wyo", input_rows, w1).astype(bf16)
        mixed = lax.all_to_all(raised_rows, "tensor", split_axis=1, concat_axis=0, tiled=True)
        mixed = mixed.reshape(blocks, owned, spread, all_rows).transpose(1, 0, 2, 3)
        mixed = mixed.reshape(owned, width, all_rows)
        linear = matrix_product("bkt,bkn->bnt", mixed, w2)
        gelu_rows = gelu_tanh(linear).astype(bf16)
        slope = gelu_slope(linear)
        lowered = matrix_product("bnt,bnk->bkt", gelu_rows, w3).astype(bf16)
        back = lax.all_to_all(lowered, "tensor", split_axis=1, concat_axis=0, tiled=True)
        back = back.reshape(blocks, owned, spread, all_rows).transpose(1, 0, 2, 3)
        back = back.reshape(owned, width, all_rows)
        return input_rows.transpose(1, 2, 0), mixed, gelu_rows, slope, back

    forward_values = forward(input_rows, w1[0], w2[0], w3[0])
    gathered, by_rows, forward_values = lax.optimization_barrier(
        (gathered, by_rows, forward_values)
    )

    weight_shapes = [
        pltpu.VMEM((devices, owned, hidden, width), bf16),
        pltpu.VMEM((devices // 2, owned * width, 2 * width), bf16),
        pltpu.VMEM((devices, owned, width, hidden), bf16),
        pltpu.VMEM((devices // 2, owned * width, 2 * width), bf16),
    ]
    copies = pltpu.SemaphoreType.DMA((owned * (5 + hidden // width),))
    row_shape = jax.ShapeDtypeStruct((blocks, rows, width), bf16)
    kept_shape = jax.ShapeDtypeStruct((blocks, 3, rows, width), bf16)
    scratch = [
        pltpu.VMEM((blocks * rows, width), f32),
        pltpu.VMEM((blocks * rows, width), f32),
        pltpu.VMEM((blocks, rows, hidden), bf16),
    ]
    last = section_count - 1
    cotangent, kept, slope, *weights = pl.pallas_call(
        functools.partial(first_body, last),
        out_shape=[row_shape, kept_shape, pltpu.VMEM((blocks, rows, hidden), f32)]
        + weight_shapes,
        in_specs=[IN_SMEM, IN_VMEM, IN_HBM, IN_HBM],
        out_specs=in_vmem(7),
        scratch_shapes=scratch + [copies],
        compiler_params=pltpu.CompilerParams(vmem_limit_bytes=28 * MIB),
        name="load_and_first_section",
    )(section, by_rows, gathered, gathered.reshape(devices // 2, 2, packed_rows, width))
    for turn in range(last, -1, -1):
        if turn < last:
            cotangent = lax.ppermute(cotangent, "section", [(turn + 1, turn)])
            cotangent, kept = pl.pallas_call(
                functools.partial(step_body, turn),
                out_shape=[row_shape, kept_shape],
                in_specs=[IN_SMEM] + in_vmem(7),
                out_specs=in_vmem(2),
                scratch_shapes=scratch,
                compiler_params=pltpu.CompilerParams(vmem_limit_bytes=8 * MIB),
                name="section_step",
            )(section, cotangent, kept, slope, *weights)

    returned = to_owners(kept.reshape(devices, owned, 3, rows, width))
    grad_inputs, *grads = pl.pallas_call(
        gradients_body,
        out_shape=[
            jax.ShapeDtypeStruct((all_rows, owned * width), bf16),
            jax.ShapeDtypeStruct((owned, width, width), f32),
            jax.ShapeDtypeStruct((owned, width, hidden), f32),
            jax.ShapeDtypeStruct((owned, hidden, width), f32),
            jax.ShapeDtypeStruct((owned, width, width), f32),
        ],
        in_specs=in_vmem(8),
        out_specs=in_vmem(5),
        compiler_params=pltpu.CompilerParams(vmem_limit_bytes=24 * MIB),
        name="gradients",
    )(returned, w1[0], w3[0], *forward_values)
    grad_inputs = grad_inputs.reshape(section_inputs.shape)
    return (grad_inputs, *[grad[None] for grad in grads])


def solution(mesh):
    in_specs = (
        P("section", None, None, "tensor"),
        P(None, None, "tensor"),
        P("section", "tensor", None, None),
        P("section", "tensor", None, None),
        P("section", "tensor", None, None),
        P("section", "tensor", None, None),
    )
    out_specs = (
        P("section", None, None, "tensor"),
        P("section", "tensor", None, None),
        P("section", "tensor", None, None),
        P("section", "tensor", None, None),
        P("section", "tensor", None, None),
    )
    return jax.shard_map(local, mesh=mesh, in_specs=in_specs, out_specs=out_specs, check_vma=False)
```

```python
import functools

import jax
import jax.numpy as jnp
from jax import lax
from jax.experimental import pallas as pl
from jax.experimental.pallas import tpu as pltpu
from jax.sharding import PartitionSpec as P

SQRT_TWO_PI = 0.7978845608028654
CUBIC_TERM = 0.044715
MIB = 2**20

IN_VMEM = pl.BlockSpec(memory_space=pltpu.VMEM)
IN_SMEM = pl.BlockSpec(memory_space=pltpu.SMEM)
IN_HBM = pl.BlockSpec(memory_space=pltpu.HBM)


def gelu_tanh(linear):
    inner = SQRT_TWO_PI * (linear + CUBIC_TERM * linear * linear * linear)
    return 0.5 * linear * (1.0 + jnp.tanh(inner))


def gelu_slope(linear):
    inner = SQRT_TWO_PI * (linear + CUBIC_TERM * linear * linear * linear)
    tangent = jnp.tanh(inner)
    return 0.5 * (1.0 + tangent) + 0.5 * linear * (1.0 - tangent * tangent) * SQRT_TWO_PI * (
        1.0 + 3.0 * CUBIC_TERM * linear * linear
    )


def matrix_product(form, left_side, right_side):
    return jnp.einsum(form, left_side, right_side, preferred_element_type=jnp.float32)


def exchange_blocks(source, target, blocks, rows):
    for row in range(rows):
        turned = source[pl.ds(row, blocks, stride=rows), :].T
        target[pl.ds(row, blocks, stride=rows), :] = jnp.concatenate(
            [turned[:blocks], turned[blocks:]], axis=1
        )


def contract_last(left_side, right_side):
    return lax.dot_general(
        left_side, right_side, (((1,), (1,)), ((), ())), preferred_element_type=jnp.float32
    )


def order_matrix(width, blocks, spread):
    grouped = lax.broadcasted_iota(jnp.int32, (width, width), 0)
    natural = lax.broadcasted_iota(jnp.int32, (width, width), 1)
    here = grouped == (natural % spread) * blocks + natural // spread
    return jnp.where(here, 1.0, 0.0).astype(jnp.bfloat16)


def prepare_body(blocks, w1_far, w2_far, w3_far, w4_far, packed, w1, w2, w3, w4, sems):
    owned, width, hidden = w2.shape
    pairs = ((w2_far, w2), (w4_far, w4), (w3_far, w3), (w1_far, w1))
    copies = [pltpu.make_async_copy(*pair, sems.at[i]) for i, pair in enumerate(pairs)]
    for copy in copies:
        copy.start()
    order = order_matrix(width, blocks, width // blocks)
    for copy in copies:
        copy.wait()
    base = 0
    for b in range(owned):
        turned = jnp.dot(order, w2[b], preferred_element_type=jnp.float32).T
        packed[pl.ds(base, hidden), :] = turned.astype(jnp.bfloat16)
        base += hidden
    for a in range(owned):
        turned = jnp.dot(order, w4[a], preferred_element_type=jnp.float32).T
        packed[pl.ds(base, width), :] = turned.astype(jnp.bfloat16)
        base += width
    for b in range(owned):
        for part in range(hidden // width):
            piece = contract_last(order, w3[b, pl.ds(part * width, width), :])
            packed[pl.ds(base, width), :] = piece.astype(jnp.bfloat16)
            base += width
    for a in range(owned):
        packed[pl.ds(base, width), :] = contract_last(order, w1[a]).astype(jnp.bfloat16)
        base += width


def loads_of(gathered, paired, second, fourth, third, first, sems):
    owned, width, hidden = third.shape[1:]
    to_second, to_fourth, to_third, to_first = [], [], [], []
    base = 0
    for half in range(owned):
        to_second.append((gathered.at[:, pl.ds(base, hidden), :], second.at[:, half]))
        base += hidden
    for target, group, start in (
        (fourth, to_fourth, base),
        (first, to_first, base + owned * (width + hidden)),
    ):
        for half in range(owned):
            for side in range(2):
                piece = paired.at[:, side, pl.ds(start + half * width, width), :]
                place = target.at[:, pl.ds(half * width, width), pl.ds(side * width, width)]
                group.append((piece, place))
    base += owned * width
    for half in range(owned):
        for part in range(hidden // width):
            place = third.at[:, half, :, pl.ds(part * width, width)]
            to_third.append((gathered.at[:, pl.ds(base, width), :], place))
            base += width
    groups, number = [], 0
    for group in (to_second, to_fourth, to_third, to_first):
        copies = []
        for source, target in group:
            copies.append(pltpu.make_async_copy(source, target, sems.at[number]))
            number += 1
        groups.append(copies)
    return groups


def start_all(copies):
    for copy in copies:
        copy.start()


def block_tiles(rows_of, tiles):
    for number in range(tiles.shape[0]):
        four = [rows_of(4 * number + i) for i in range(4)]
        empty = jnp.zeros_like(four[0])
        spread = [
            jnp.concatenate([value, empty] if i % 2 == 0 else [empty, value], axis=1)
            for i, value in enumerate(four)
        ]
        product = jnp.dot(
            jnp.concatenate(spread, axis=0), tiles[number], preferred_element_type=jnp.float32
        )
        pair = 2 * four[0].shape[0]
        width = four[0].shape[1]
        yield 4 * number, product[:pair, :width]
        yield 4 * number + 2, product[pair:, width:]


def wait_all(copies):
    for copy in copies:
        copy.wait()


def first_body(
    turn,
    section,
    raised,
    targets,
    gathered,
    paired,
    result,
    kept,
    slope,
    second,
    fourth,
    third,
    first,
    rows_in,
    rows_out,
    grad_lin,
    sems,
):
    blocks, rows, width = raised.shape
    owned = third.shape[1]
    to_second, to_fourth, to_third, to_first = loads_of(
        gathered, paired, second, fourth, third, first, sems
    )
    start_all(to_second + to_fourth)
    rows_in[...] = raised[...].astype(jnp.float32).reshape(blocks * rows, width)
    exchange_blocks(rows_in, rows_out, blocks, rows)
    wait_all(to_second)
    start_all(to_third + to_first)
    for b in range(blocks):
        mixed = rows_out[pl.ds(b * rows, rows), :].astype(jnp.bfloat16)
        slope[b] = gelu_slope(contract_last(mixed, second[b // owned, b % owned]))

    @pl.when(section[0] != turn)
    def _():
        wait_all(to_fourth + to_third + to_first)
        result[...] = targets[...]
        for kind in range(kept.shape[1]):
            kept[:, kind] = targets[...]

    @pl.when(section[0] == turn)
    def _():
        result[...] = targets[...]
        one_section(
            result,
            kept,
            slope,
            second,
            fourth,
            third,
            first,
            rows_in,
            rows_out,
            grad_lin,
            (to_fourth, to_third, to_first),
        )


def one_section(
    result,
    kept,
    slope,
    second,
    fourth,
    third,
    first,
    rows_in,
    rows_out,
    grad_lin,
    loads=((), (), ()),
):
    blocks, rows, width = result.shape
    owned = third.shape[1]
    kept[:, 0] = result[...]
    wait_all(loads[0])
    for a, product in block_tiles(lambda a: kept[a, 0], fourth):
        rows_in[pl.ds(a * rows, 2 * rows), :] = product
    exchange_blocks(rows_in, rows_out, blocks, rows)
    kept[:, 1] = rows_out[...].reshape(blocks, rows, width).astype(jnp.bfloat16)
    wait_all(loads[1])
    for b in range(blocks):
        grad_hid = jnp.dot(
            kept[b, 1], third[b // owned, b % owned], preferred_element_type=jnp.float32
        )
        grad_lin[b] = (grad_hid * slope[b]).astype(jnp.bfloat16)
    for b in range(blocks):
        rows_in[pl.ds(b * rows, rows), :] = jnp.dot(
            grad_lin[b], second[b // owned, b % owned], preferred_element_type=jnp.float32
        )
    exchange_blocks(rows_in, rows_out, blocks, rows)
    kept[:, 2] = rows_out[...].reshape(blocks, rows, width).astype(jnp.bfloat16)
    wait_all(loads[2])
    for a, product in block_tiles(lambda a: kept[a, 2], first):
        for i in range(2):
            total = kept[a + i, 0].astype(jnp.float32) + product[i * rows : (i + 1) * rows]
            result[a + i] = total.astype(jnp.bfloat16)


def step_body(
    turn,
    section,
    cotangent,
    old_kept,
    slope,
    second,
    fourth,
    third,
    first,
    result,
    kept,
    rows_in,
    rows_out,
    grad_lin,
):
    result[...] = cotangent[...]

    @pl.when(section[0] != turn)
    def _():
        kept[...] = old_kept[...]

    @pl.when(section[0] == turn)
    def _():
        one_section(
            result, kept, slope, second, fourth, third, first, rows_in, rows_out, grad_lin
        )


def reload_body(gathered, paired, second, fourth, third, first, sems):
    groups = loads_of(gathered, paired, second, fourth, third, first, sems)
    for copies in groups:
        start_all(copies)
    for copies in groups:
        wait_all(copies)


def gradients_body(
    returned,
    w1,
    w3,
    inputs,
    mixed,
    gelu_rows,
    slope,
    handed_back,
    grad_inputs,
    grad_w1,
    grad_w2,
    grad_w3,
    grad_w4,
):
    devices, owned, _, rows, width = returned.shape
    order = order_matrix(width, devices * owned, width // (devices * owned))

    def rows_of(block, kind):
        value = returned[:, block, kind].astype(jnp.float32)
        return value.reshape(devices * rows, width)

    def in_natural_order(value):
        return jnp.dot(
            value.astype(jnp.bfloat16), order, preferred_element_type=jnp.float32
        ).astype(jnp.bfloat16)

    for a in range(owned):
        gy = rows_of(a, 0)
        gu = in_natural_order(rows_of(a, 2))
        grad_inputs[:, a * width : (a + 1) * width] = (gy + contract_last(gu, w1[a])).astype(
            jnp.bfloat16
        )
        grad_w1[a] = jnp.dot(inputs[a], gu, preferred_element_type=jnp.float32)
        grad_w4[a] = jnp.dot(
            handed_back[a], gy.astype(jnp.bfloat16), preferred_element_type=jnp.float32
        )
    for b in range(owned):
        gv = in_natural_order(rows_of(b, 1))
        grad_lin = (contract_last(w3[b], gv) * slope[b]).astype(jnp.bfloat16)
        grad_w2[b] = contract_last(mixed[b], grad_lin)
        grad_w3[b] = jnp.dot(gelu_rows[b], gv, preferred_element_type=jnp.float32)


def in_vmem(count):
    return [IN_VMEM] * count


def to_owners(value):
    return lax.all_to_all(value, "tensor", split_axis=0, concat_axis=0, tiled=True)


def local(section_inputs, out_grad, w1, w2, w3, w4):
    devices = lax.axis_size("tensor")
    section_count = lax.axis_size("section")
    section = lax.axis_index("section").astype(jnp.int32).reshape(1)
    all_rows = section_inputs.shape[1] * section_inputs.shape[2]
    owned, width, hidden = w2.shape[1:]
    blocks = owned * devices
    spread = width // blocks
    rows = all_rows // devices
    packed_rows = owned * (2 * hidden + 2 * width)
    bf16, f32 = jnp.bfloat16, jnp.float32

    packed = pl.pallas_call(
        functools.partial(prepare_body, blocks),
        out_shape=jax.ShapeDtypeStruct((packed_rows, width), bf16),
        in_specs=[IN_HBM] * 4,
        out_specs=IN_VMEM,
        scratch_shapes=[pltpu.VMEM(w.shape[1:], bf16) for w in (w1, w2, w3, w4)]
        + [pltpu.SemaphoreType.DMA((4,))],
        compiler_params=pltpu.CompilerParams(vmem_limit_bytes=60 * MIB),
        name="prepare_weights",
    )(w1[0], w2[0], w3[0], w4[0])
    gathered = lax.all_gather(packed, "tensor", axis=0, tiled=False)

    input_rows = section_inputs[0].reshape(all_rows, owned, width)
    first_local = packed[packed_rows - owned * width :].reshape(owned, width, width)
    raised = matrix_product("tac,apc->atp", input_rows, first_local).astype(bf16)
    raised = raised.reshape(owned, devices, rows, width).transpose(1, 0, 2, 3)
    raised = to_owners(raised).reshape(blocks, rows, width)
    share = rows * owned // section_count
    targets = out_grad.reshape(devices, section_count, share, width)
    targets = lax.dynamic_index_in_dim(targets, section[0], axis=1, keepdims=False)
    targets = lax.all_gather(to_owners(targets), "section", axis=1, tiled=False)
    targets = targets.reshape(devices, rows, owned, width).transpose(0, 2, 1, 3)
    targets = targets.reshape(blocks, rows, width)

    def forward(input_rows, w1, w2, w3):
        raised_rows = matrix_product("owz,wzy->wyo", input_rows, w1).astype(bf16)
        mixed = lax.all_to_all(raised_rows, "tensor", split_axis=1, concat_axis=0, tiled=True)
        mixed = mixed.reshape(blocks, owned, spread, all_rows).transpose(1, 0, 2, 3)
        mixed = mixed.reshape(owned, width, all_rows)
        linear = matrix_product("bkt,bkn->bnt", mixed, w2)
        gelu_rows = gelu_tanh(linear).astype(bf16)
        slope = gelu_slope(linear)
        lowered = matrix_product("bnt,bnk->bkt", gelu_rows, w3).astype(bf16)
        back = lax.all_to_all(lowered, "tensor", split_axis=1, concat_axis=0, tiled=True)
        back = back.reshape(blocks, owned, spread, all_rows).transpose(1, 0, 2, 3)
        back = back.reshape(owned, width, all_rows)
        return input_rows.transpose(1, 2, 0), mixed, gelu_rows, slope, back

    weight_shapes = [
        pltpu.VMEM((devices, owned, hidden, width), bf16),
        pltpu.VMEM((devices // 2, owned * width, 2 * width), bf16),
        pltpu.VMEM((devices, owned, width, hidden), bf16),
        pltpu.VMEM((devices // 2, owned * width, 2 * width), bf16),
    ]
    copies = pltpu.SemaphoreType.DMA((owned * (5 + hidden // width),))
    row_shape = jax.ShapeDtypeStruct((blocks, rows, width), bf16)
    kept_shape = jax.ShapeDtypeStruct((blocks, 3, rows, width), bf16)
    scratch = [
        pltpu.VMEM((blocks * rows, width), f32),
        pltpu.VMEM((blocks * rows, width), f32),
        pltpu.VMEM((blocks, rows, hidden), bf16),
    ]
    last = section_count - 1
    gathered, raised, targets = lax.optimization_barrier((gathered, raised, targets))
    cotangent, kept, slope, *weights = pl.pallas_call(
        functools.partial(first_body, last),
        out_shape=[row_shape, kept_shape, pltpu.VMEM((blocks, rows, hidden), f32)]
        + weight_shapes,
        in_specs=[IN_SMEM, IN_VMEM, IN_VMEM, IN_HBM, IN_HBM],
        out_specs=in_vmem(7),
        scratch_shapes=scratch + [copies],
        compiler_params=pltpu.CompilerParams(vmem_limit_bytes=28 * MIB),
        name="load_and_first_section",
    )(section, raised, targets, gathered, gathered.reshape(devices // 2, 2, packed_rows, width))
    for turn in range(last, -1, -1):
        if turn < last:
            cotangent = lax.ppermute(cotangent, "section", [(turn + 1, turn)])
            cotangent, kept = pl.pallas_call(
                functools.partial(step_body, turn),
                out_shape=[row_shape, kept_shape],
                in_specs=[IN_SMEM] + in_vmem(7),
                out_specs=in_vmem(2),
                scratch_shapes=scratch,
                compiler_params=pltpu.CompilerParams(vmem_limit_bytes=8 * MIB),
                name="section_step",
            )(section, cotangent, kept, slope, *weights)
        if turn == section_count // 2:
            kept, given = lax.optimization_barrier((kept, (input_rows, w1[0], w2[0], w3[0])))
            nothing = jax.tree.map(
                lambda value: jnp.zeros(value.shape, value.dtype), jax.eval_shape(forward, *given)
            )
            forward_values = lax.cond(
                section[0] >= 0, lambda *given: forward(*given), lambda *given: nothing, *given
            )
            gathered, forward_values = lax.optimization_barrier((gathered, forward_values))
            weights = pl.pallas_call(
                reload_body,
                out_shape=weight_shapes,
                in_specs=[IN_HBM, IN_HBM],
                out_specs=in_vmem(4),
                scratch_shapes=[copies],
                compiler_params=pltpu.CompilerParams(vmem_limit_bytes=28 * MIB),
                name="load_again",
            )(gathered, gathered.reshape(devices // 2, 2, packed_rows, width))

    returned = to_owners(kept.reshape(devices, owned, 3, rows, width))
    grad_inputs, *grads = pl.pallas_call(
        gradients_body,
        out_shape=[
            jax.ShapeDtypeStruct((all_rows, owned * width), bf16),
            jax.ShapeDtypeStruct((owned, width, width), f32),
            jax.ShapeDtypeStruct((owned, width, hidden), f32),
            jax.ShapeDtypeStruct((owned, hidden, width), f32),
            jax.ShapeDtypeStruct((owned, width, width), f32),
        ],
        in_specs=in_vmem(8),
        out_specs=in_vmem(5),
        compiler_params=pltpu.CompilerParams(vmem_limit_bytes=24 * MIB),
        name="gradients",
    )(returned, w1[0], w3[0], *forward_values)
    grad_inputs = grad_inputs.reshape(section_inputs.shape)
    return (grad_inputs, *[grad[None] for grad in grads])


def solution(mesh):
    in_specs = (
        P("section", None, None, "tensor"),
        P(None, None, "tensor"),
        P("section", "tensor", None, None),
        P("section", "tensor", None, None),
        P("section", "tensor", None, None),
        P("section", "tensor", None, None),
    )
    out_specs = (
        P("section", None, None, "tensor"),
        P("section", "tensor", None, None),
        P("section", "tensor", None, None),
        P("section", "tensor", None, None),
        P("section", "tensor", None, None),
    )
    return jax.shard_map(local, mesh=mesh, in_specs=in_specs, out_specs=out_specs, check_vma=False)
```

```python
import functools

import jax
import jax.numpy as jnp
from jax import lax
from jax.experimental import pallas as pl
from jax.experimental.pallas import tpu as pltpu
from jax.sharding import PartitionSpec as P

SQRT_TWO_PI = 0.7978845608028654
CUBIC_TERM = 0.044715
MIB = 2**20

IN_VMEM = pl.BlockSpec(memory_space=pltpu.VMEM)
IN_SMEM = pl.BlockSpec(memory_space=pltpu.SMEM)
IN_HBM = pl.BlockSpec(memory_space=pltpu.HBM)


def gelu_tanh(linear):
    inner = SQRT_TWO_PI * (linear + CUBIC_TERM * linear * linear * linear)
    return 0.5 * linear * (1.0 + jnp.tanh(inner))


def gelu_slope(linear):
    inner = SQRT_TWO_PI * (linear + CUBIC_TERM * linear * linear * linear)
    tangent = jnp.tanh(inner)
    return 0.5 * (1.0 + tangent) + 0.5 * linear * (1.0 - tangent * tangent) * SQRT_TWO_PI * (
        1.0 + 3.0 * CUBIC_TERM * linear * linear
    )


def matrix_product(form, left_side, right_side):
    return jnp.einsum(form, left_side, right_side, preferred_element_type=jnp.float32)


def exchange_blocks(source, target, blocks, rows):
    for row in range(0, rows, 2):
        pair = [source[pl.ds(row + i, blocks, stride=rows), :] for i in range(2)]
        turned = jnp.concatenate(pair, axis=0).T
        for i in range(2):
            lanes = slice(i * blocks, (i + 1) * blocks)
            target[pl.ds(row + i, blocks, stride=rows), :] = jnp.concatenate(
                [turned[:blocks, lanes], turned[blocks:, lanes]], axis=1
            )


def contract_last(left_side, right_side):
    return lax.dot_general(
        left_side, right_side, (((1,), (1,)), ((), ())), preferred_element_type=jnp.float32
    )


def order_matrix(width, blocks, spread):
    grouped = lax.broadcasted_iota(jnp.int32, (width, width), 0)
    natural = lax.broadcasted_iota(jnp.int32, (width, width), 1)
    here = grouped == (natural % spread) * blocks + natural // spread
    return jnp.where(here, 1.0, 0.0).astype(jnp.bfloat16)


def prepare_body(blocks, w1_far, w2_far, w3_far, w4_far, packed, w1, w2, w3, w4, sems):
    owned, width, hidden = w2.shape
    pairs = ((w2_far, w2), (w4_far, w4), (w3_far, w3), (w1_far, w1))
    copies = [pltpu.make_async_copy(*pair, sems.at[i]) for i, pair in enumerate(pairs)]
    for copy in copies:
        copy.start()
    order = order_matrix(width, blocks, width // blocks)
    for copy in copies:
        copy.wait()
    base = 0
    for b in range(owned):
        turned = jnp.dot(order, w2[b], preferred_element_type=jnp.float32).T
        packed[pl.ds(base, hidden), :] = turned.astype(jnp.bfloat16)
        base += hidden
    for a in range(owned):
        turned = jnp.dot(order, w4[a], preferred_element_type=jnp.float32).T
        packed[pl.ds(base, width), :] = turned.astype(jnp.bfloat16)
        base += width
    for b in range(owned):
        for part in range(hidden // width):
            piece = contract_last(order, w3[b, pl.ds(part * width, width), :])
            packed[pl.ds(base, width), :] = piece.astype(jnp.bfloat16)
            base += width
    for a in range(owned):
        packed[pl.ds(base, width), :] = contract_last(order, w1[a]).astype(jnp.bfloat16)
        base += width


def loads_of(gathered, paired, second, fourth, third, first, sems):
    owned, width, hidden = third.shape[1:]
    to_second, to_fourth, to_third, to_first = [], [], [], []
    base = 0
    for half in range(owned):
        to_second.append((gathered.at[:, pl.ds(base, hidden), :], second.at[:, half]))
        base += hidden
    for target, group, start in (
        (fourth, to_fourth, base),
        (first, to_first, base + owned * (width + hidden)),
    ):
        for half in range(owned):
            for side in range(2):
                piece = paired.at[:, side, pl.ds(start + half * width, width), :]
                place = target.at[:, pl.ds(half * width, width), pl.ds(side * width, width)]
                group.append((piece, place))
    base += owned * width
    for half in range(owned):
        for part in range(hidden // width):
            place = third.at[:, half, :, pl.ds(part * width, width)]
            to_third.append((gathered.at[:, pl.ds(base, width), :], place))
            base += width
    groups, number = [], 0
    for group in (to_second, to_fourth, to_third, to_first):
        copies = []
        for source, target in group:
            copies.append(pltpu.make_async_copy(source, target, sems.at[number]))
            number += 1
        groups.append(copies)
    return groups


def start_all(copies):
    for copy in copies:
        copy.start()


def block_tiles(rows_of, tiles):
    for number in range(tiles.shape[0]):
        four = [rows_of(4 * number + i) for i in range(4)]
        empty = jnp.zeros_like(four[0])
        spread = [
            jnp.concatenate([value, empty] if i % 2 == 0 else [empty, value], axis=1)
            for i, value in enumerate(four)
        ]
        product = jnp.dot(
            jnp.concatenate(spread, axis=0), tiles[number], preferred_element_type=jnp.float32
        )
        pair = 2 * four[0].shape[0]
        width = four[0].shape[1]
        yield 4 * number, product[:pair, :width]
        yield 4 * number + 2, product[pair:, width:]


def wait_all(copies):
    for copy in copies:
        copy.wait()


def first_body(
    turn,
    section,
    raised,
    targets,
    gathered,
    paired,
    result,
    kept,
    slope,
    second,
    fourth,
    third,
    first,
    rows_in,
    rows_out,
    grad_lin,
    sems,
):
    blocks, rows, width = raised.shape
    owned = third.shape[1]
    to_second, to_fourth, to_third, to_first = loads_of(
        gathered, paired, second, fourth, third, first, sems
    )
    start_all(to_fourth + to_second)

    @pl.when(section[0] == turn)
    def _():
        wait_all(to_fourth)
        middle_gradient(targets, kept, fourth, rows_in, rows_out)

    rows_in[...] = raised[...].astype(jnp.float32).reshape(blocks * rows, width)
    exchange_blocks(rows_in, rows_out, blocks, rows)
    wait_all(to_second)
    start_all(to_third + to_first)
    for b in range(blocks):
        mixed = rows_out[pl.ds(b * rows, rows), :].astype(jnp.bfloat16)
        slope[b] = gelu_slope(contract_last(mixed, second[b // owned, b % owned]))

    @pl.when(section[0] != turn)
    def _():
        wait_all(to_fourth + to_third + to_first)

    @pl.when(section[0] == turn)
    def _():
        wait_all(to_third + to_first)
        input_gradient(
            targets, result, kept, slope, second, third, first, rows_in, rows_out, grad_lin
        )


def middle_gradient(cotangent, kept, fourth, rows_in, rows_out):
    blocks, rows, width = cotangent.shape
    kept[:, 0] = cotangent[...]
    for a, product in block_tiles(lambda a: cotangent[a], fourth):
        rows_in[pl.ds(a * rows, 2 * rows), :] = product
    exchange_blocks(rows_in, rows_out, blocks, rows)
    kept[:, 1] = rows_out[...].reshape(blocks, rows, width).astype(jnp.bfloat16)


def input_gradient(
    cotangent, result, kept, slope, second, third, first, rows_in, rows_out, grad_lin
):
    blocks, rows, width = cotangent.shape
    owned = third.shape[1]
    for b in range(blocks):
        grad_hid = jnp.dot(
            kept[b, 1], third[b // owned, b % owned], preferred_element_type=jnp.float32
        )
        grad_lin[b] = (grad_hid * slope[b]).astype(jnp.bfloat16)
    for b in range(blocks):
        rows_in[pl.ds(b * rows, rows), :] = jnp.dot(
            grad_lin[b], second[b // owned, b % owned], preferred_element_type=jnp.float32
        )
    exchange_blocks(rows_in, rows_out, blocks, rows)
    kept[:, 2] = rows_out[...].reshape(blocks, rows, width).astype(jnp.bfloat16)
    for a, product in block_tiles(lambda a: kept[a, 2], first):
        for i in range(2):
            total = cotangent[a + i].astype(jnp.float32) + product[i * rows : (i + 1) * rows]
            result[a + i] = total.astype(jnp.bfloat16)


def step_body(
    turn,
    section,
    cotangent,
    old_kept,
    slope,
    second,
    fourth,
    third,
    first,
    result,
    kept,
    rows_in,
    rows_out,
    grad_lin,
):
    @pl.when(section[0] != turn)
    def _():
        kept[...] = old_kept[...]

    @pl.when(section[0] == turn)
    def _():
        middle_gradient(cotangent, kept, fourth, rows_in, rows_out)
        input_gradient(
            cotangent, result, kept, slope, second, third, first, rows_in, rows_out, grad_lin
        )


def reload_body(gathered, paired, second, fourth, third, first, sems):
    groups = loads_of(gathered, paired, second, fourth, third, first, sems)
    for copies in groups:
        start_all(copies)
    for copies in groups:
        wait_all(copies)


def gradients_body(
    returned,
    w1,
    w3,
    inputs,
    mixed,
    gelu_rows,
    slope,
    handed_back,
    grad_inputs,
    grad_w1,
    grad_w2,
    grad_w3,
    grad_w4,
):
    devices, owned, _, rows, width = returned.shape
    order = order_matrix(width, devices * owned, width // (devices * owned))

    def rows_of(block, kind):
        value = returned[:, block, kind].astype(jnp.float32)
        return value.reshape(devices * rows, width)

    def in_natural_order(value):
        return jnp.dot(
            value.astype(jnp.bfloat16), order, preferred_element_type=jnp.float32
        ).astype(jnp.bfloat16)

    for a in range(owned):
        gy = rows_of(a, 0)
        gu = in_natural_order(rows_of(a, 2))
        grad_inputs[:, a * width : (a + 1) * width] = (gy + contract_last(gu, w1[a])).astype(
            jnp.bfloat16
        )
        grad_w1[a] = jnp.dot(inputs[a], gu, preferred_element_type=jnp.float32)
        grad_w4[a] = jnp.dot(
            handed_back[a], gy.astype(jnp.bfloat16), preferred_element_type=jnp.float32
        )
    for b in range(owned):
        gv = in_natural_order(rows_of(b, 1))
        grad_lin = (contract_last(w3[b], gv) * slope[b]).astype(jnp.bfloat16)
        grad_w2[b] = contract_last(mixed[b], grad_lin)
        grad_w3[b] = jnp.dot(gelu_rows[b], gv, preferred_element_type=jnp.float32)


def in_vmem(count):
    return [IN_VMEM] * count


def to_owners(value):
    return lax.all_to_all(value, "tensor", split_axis=0, concat_axis=0, tiled=True)


def local(section_inputs, out_grad, w1, w2, w3, w4):
    devices = lax.axis_size("tensor")
    section_count = lax.axis_size("section")
    section = lax.axis_index("section").astype(jnp.int32).reshape(1)
    all_rows = section_inputs.shape[1] * section_inputs.shape[2]
    owned, width, hidden = w2.shape[1:]
    blocks = owned * devices
    spread = width // blocks
    rows = all_rows // devices
    packed_rows = owned * (2 * hidden + 2 * width)
    bf16, f32 = jnp.bfloat16, jnp.float32

    packed = pl.pallas_call(
        functools.partial(prepare_body, blocks),
        out_shape=jax.ShapeDtypeStruct((packed_rows, width), bf16),
        in_specs=[IN_HBM] * 4,
        out_specs=IN_VMEM,
        scratch_shapes=[pltpu.VMEM(w.shape[1:], bf16) for w in (w1, w2, w3, w4)]
        + [pltpu.SemaphoreType.DMA((4,))],
        compiler_params=pltpu.CompilerParams(vmem_limit_bytes=60 * MIB),
        name="prepare_weights",
    )(w1[0], w2[0], w3[0], w4[0])
    gathered = lax.all_gather(packed, "tensor", axis=0, tiled=False)

    input_rows = section_inputs[0].reshape(all_rows, owned, width)
    first_local = packed[packed_rows - owned * width :].reshape(owned, width, width)
    raised = matrix_product("tac,apc->atp", input_rows, first_local).astype(bf16)
    raised = raised.reshape(owned, devices, rows, width).transpose(1, 0, 2, 3)
    raised = to_owners(raised).reshape(blocks, rows, width)
    share = rows * owned // section_count
    targets = out_grad.reshape(devices, section_count, share, width)
    targets = lax.dynamic_index_in_dim(targets, section[0], axis=1, keepdims=False)
    targets = lax.all_gather(to_owners(targets), "section", axis=1, tiled=False)
    targets = targets.reshape(devices, rows, owned, width).transpose(0, 2, 1, 3)
    targets = targets.reshape(blocks, rows, width)

    def forward(input_rows, w1, w2, w3):
        raised_rows = matrix_product("owz,wzy->wyo", input_rows, w1).astype(bf16)
        mixed = lax.all_to_all(raised_rows, "tensor", split_axis=1, concat_axis=0, tiled=True)
        mixed = mixed.reshape(blocks, owned, spread, all_rows).transpose(1, 0, 2, 3)
        mixed = mixed.reshape(owned, width, all_rows)
        linear = matrix_product("bkt,bkn->bnt", mixed, w2)
        gelu_rows = gelu_tanh(linear).astype(bf16)
        slope = gelu_slope(linear)
        lowered = matrix_product("bnt,bnk->bkt", gelu_rows, w3).astype(bf16)
        back = lax.all_to_all(lowered, "tensor", split_axis=1, concat_axis=0, tiled=True)
        back = back.reshape(blocks, owned, spread, all_rows).transpose(1, 0, 2, 3)
        back = back.reshape(owned, width, all_rows)
        return input_rows.transpose(1, 2, 0), mixed, gelu_rows, slope, back

    weight_shapes = [
        pltpu.VMEM((devices, owned, hidden, width), bf16),
        pltpu.VMEM((devices // 2, owned * width, 2 * width), bf16),
        pltpu.VMEM((devices, owned, width, hidden), bf16),
        pltpu.VMEM((devices // 2, owned * width, 2 * width), bf16),
    ]
    copies = pltpu.SemaphoreType.DMA((owned * (5 + hidden // width),))
    row_shape = jax.ShapeDtypeStruct((blocks, rows, width), bf16)
    kept_shape = jax.ShapeDtypeStruct((blocks, 3, rows, width), bf16)
    scratch = [
        pltpu.VMEM((blocks * rows, width), f32),
        pltpu.VMEM((blocks * rows, width), f32),
        pltpu.VMEM((blocks, rows, hidden), bf16),
    ]
    last = section_count - 1
    gathered, raised, targets = lax.optimization_barrier((gathered, raised, targets))
    cotangent, kept, slope, *weights = pl.pallas_call(
        functools.partial(first_body, last),
        out_shape=[row_shape, kept_shape, pltpu.VMEM((blocks, rows, hidden), f32)]
        + weight_shapes,
        in_specs=[IN_SMEM, IN_VMEM, IN_VMEM, IN_HBM, IN_HBM],
        out_specs=in_vmem(7),
        scratch_shapes=scratch + [copies],
        compiler_params=pltpu.CompilerParams(vmem_limit_bytes=28 * MIB),
        name="load_and_first_section",
    )(section, raised, targets, gathered, gathered.reshape(devices // 2, 2, packed_rows, width))
    for turn in range(last, -1, -1):
        if turn < last:
            cotangent = lax.ppermute(cotangent, "section", [(turn + 1, turn)])
            cotangent, kept = pl.pallas_call(
                functools.partial(step_body, turn),
                out_shape=[row_shape, kept_shape],
                in_specs=[IN_SMEM] + in_vmem(7),
                out_specs=in_vmem(2),
                scratch_shapes=scratch,
                compiler_params=pltpu.CompilerParams(vmem_limit_bytes=8 * MIB),
                name="section_step",
            )(section, cotangent, kept, slope, *weights)
        if turn == section_count // 2:
            kept, given = lax.optimization_barrier((kept, (input_rows, w1[0], w2[0], w3[0])))
            nothing = jax.tree.map(
                lambda value: jnp.zeros(value.shape, value.dtype), jax.eval_shape(forward, *given)
            )
            forward_values = lax.cond(
                section[0] >= 0, lambda *given: forward(*given), lambda *given: nothing, *given
            )
            gathered, forward_values = lax.optimization_barrier((gathered, forward_values))
            weights = pl.pallas_call(
                reload_body,
                out_shape=weight_shapes,
                in_specs=[IN_HBM, IN_HBM],
                out_specs=in_vmem(4),
                scratch_shapes=[copies],
                compiler_params=pltpu.CompilerParams(vmem_limit_bytes=28 * MIB),
                name="load_again",
            )(gathered, gathered.reshape(devices // 2, 2, packed_rows, width))

    returned = to_owners(kept.reshape(devices, owned, 3, rows, width))
    grad_inputs, *grads = pl.pallas_call(
        gradients_body,
        out_shape=[
            jax.ShapeDtypeStruct((all_rows, owned * width), bf16),
            jax.ShapeDtypeStruct((owned, width, width), f32),
            jax.ShapeDtypeStruct((owned, width, hidden), f32),
            jax.ShapeDtypeStruct((owned, hidden, width), f32),
            jax.ShapeDtypeStruct((owned, width, width), f32),
        ],
        in_specs=in_vmem(8),
        out_specs=in_vmem(5),
        compiler_params=pltpu.CompilerParams(vmem_limit_bytes=24 * MIB),
        name="gradients",
    )(returned, w1[0], w3[0], *forward_values)
    grad_inputs = grad_inputs.reshape(section_inputs.shape)
    return (grad_inputs, *[grad[None] for grad in grads])


def solution(mesh):
    in_specs = (
        P("section", None, None, "tensor"),
        P(None, None, "tensor"),
        P("section", "tensor", None, None),
        P("section", "tensor", None, None),
        P("section", "tensor", None, None),
        P("section", "tensor", None, None),
    )
    out_specs = (
        P("section", None, None, "tensor"),
        P("section", "tensor", None, None),
        P("section", "tensor", None, None),
        P("section", "tensor", None, None),
        P("section", "tensor", None, None),
    )
    return jax.shard_map(local, mesh=mesh, in_specs=in_specs, out_specs=out_specs, check_vma=False)
```

```python
import functools

import jax
import jax.numpy as jnp
from jax import lax
from jax.experimental import pallas as pl
from jax.experimental.pallas import tpu as pltpu
from jax.sharding import PartitionSpec as P

SQRT_TWO_PI = 0.7978845608028654
CUBIC_TERM = 0.044715
MIB = 2**20

IN_VMEM = pl.BlockSpec(memory_space=pltpu.VMEM)
IN_SMEM = pl.BlockSpec(memory_space=pltpu.SMEM)
IN_HBM = pl.BlockSpec(memory_space=pltpu.HBM)


def gelu_tanh(linear):
    inner = SQRT_TWO_PI * (linear + CUBIC_TERM * linear * linear * linear)
    return 0.5 * linear * (1.0 + jnp.tanh(inner))


def gelu_slope(linear):
    inner = SQRT_TWO_PI * (linear + CUBIC_TERM * linear * linear * linear)
    tangent = jnp.tanh(inner)
    return 0.5 * (1.0 + tangent) + 0.5 * linear * (1.0 - tangent * tangent) * SQRT_TWO_PI * (
        1.0 + 3.0 * CUBIC_TERM * linear * linear
    )


def matrix_product(form, left_side, right_side):
    return jnp.einsum(form, left_side, right_side, preferred_element_type=jnp.float32)


def exchange_blocks(source, target, blocks, rows):
    for row in range(0, rows, 2):
        pair = [source[pl.ds(row + i, blocks, stride=rows), :] for i in range(2)]
        turned = jnp.concatenate(pair, axis=0).T
        for i in range(2):
            lanes = slice(i * blocks, (i + 1) * blocks)
            target[pl.ds(row + i, blocks, stride=rows), :] = jnp.concatenate(
                [turned[:blocks, lanes], turned[blocks:, lanes]], axis=1
            )


def contract_last(left_side, right_side):
    return lax.dot_general(
        left_side, right_side, (((1,), (1,)), ((), ())), preferred_element_type=jnp.float32
    )


def order_matrix(width, blocks, spread):
    grouped = lax.broadcasted_iota(jnp.int32, (width, width), 0)
    natural = lax.broadcasted_iota(jnp.int32, (width, width), 1)
    here = grouped == (natural % spread) * blocks + natural // spread
    return jnp.where(here, 1.0, 0.0).astype(jnp.bfloat16)


def prepare_body(blocks, w1_far, w2_far, w3_far, w4_far, packed, w1, w2, w3, w4, sems):
    owned, width, hidden = w2.shape
    pairs = ((w2_far, w2), (w4_far, w4), (w3_far, w3), (w1_far, w1))
    copies = [pltpu.make_async_copy(*pair, sems.at[i]) for i, pair in enumerate(pairs)]
    for copy in copies:
        copy.start()
    order = order_matrix(width, blocks, width // blocks)
    for copy in copies:
        copy.wait()
    base = 0
    for b in range(owned):
        turned = jnp.dot(order, w2[b], preferred_element_type=jnp.float32).T
        packed[pl.ds(base, hidden), :] = turned.astype(jnp.bfloat16)
        base += hidden
    for a in range(owned):
        turned = jnp.dot(order, w4[a], preferred_element_type=jnp.float32).T
        packed[pl.ds(base, width), :] = turned.astype(jnp.bfloat16)
        base += width
    for b in range(owned):
        for part in range(hidden // width):
            piece = contract_last(order, w3[b, pl.ds(part * width, width), :])
            packed[pl.ds(base, width), :] = piece.astype(jnp.bfloat16)
            base += width
    for a in range(owned):
        packed[pl.ds(base, width), :] = contract_last(order, w1[a]).astype(jnp.bfloat16)
        base += width


def loads_of(gathered, paired, second, fourth, third, first, sems):
    owned, width, hidden = third.shape[1:]
    to_second, to_fourth, to_third, to_first = [], [], [], []
    base = 0
    for half in range(owned):
        to_second.append((gathered.at[:, pl.ds(base, hidden), :], second.at[:, half]))
        base += hidden
    for target, group, start in (
        (fourth, to_fourth, base),
        (first, to_first, base + owned * (width + hidden)),
    ):
        for half in range(owned):
            for side in range(2):
                piece = paired.at[:, side, pl.ds(start + half * width, width), :]
                place = target.at[:, pl.ds(half * width, width), pl.ds(side * width, width)]
                group.append((piece, place))
    base += owned * width
    for half in range(owned):
        for part in range(hidden // width):
            place = third.at[:, half, :, pl.ds(part * width, width)]
            to_third.append((gathered.at[:, pl.ds(base, width), :], place))
            base += width
    groups, number = [], 0
    for group in (to_second, to_fourth, to_third, to_first):
        copies = []
        for source, target in group:
            copies.append(pltpu.make_async_copy(source, target, sems.at[number]))
            number += 1
        groups.append(copies)
    return groups


def start_all(copies):
    for copy in copies:
        copy.start()


def block_tiles(rows_of, tiles):
    for number in range(tiles.shape[0]):
        four = [rows_of(4 * number + i) for i in range(4)]
        empty = jnp.zeros_like(four[0])
        spread = [
            jnp.concatenate([value, empty] if i % 2 == 0 else [empty, value], axis=1)
            for i, value in enumerate(four)
        ]
        product = jnp.dot(
            jnp.concatenate(spread, axis=0), tiles[number], preferred_element_type=jnp.float32
        )
        pair = 2 * four[0].shape[0]
        width = four[0].shape[1]
        yield 4 * number, product[:pair, :width]
        yield 4 * number + 2, product[pair:, width:]


def wait_all(copies):
    for copy in copies:
        copy.wait()


def first_body(
    turn,
    section,
    raised,
    targets,
    gathered,
    paired,
    result,
    kept,
    slope,
    second,
    fourth,
    third,
    first,
    rows_in,
    rows_out,
    grad_lin,
    sems,
):
    blocks, rows, width = raised.shape
    owned = third.shape[1]
    to_second, to_fourth, to_third, to_first = loads_of(
        gathered, paired, second, fourth, third, first, sems
    )
    start_all(to_fourth + to_second)

    @pl.when(section[0] == turn)
    def _():
        wait_all(to_fourth)
        middle_gradient(targets, kept, fourth, rows_in, rows_out)

    rows_in[...] = raised[...].astype(jnp.float32).reshape(blocks * rows, width)
    exchange_blocks(rows_in, rows_out, blocks, rows)
    start_all(to_third + to_first)
    wait_all(to_second)
    for b in range(blocks):
        mixed = rows_out[pl.ds(b * rows, rows), :].astype(jnp.bfloat16)
        slope[b] = gelu_slope(contract_last(mixed, second[b // owned, b % owned]))

    @pl.when(section[0] != turn)
    def _():
        wait_all(to_fourth + to_third + to_first)

    @pl.when(section[0] == turn)
    def _():
        wait_all(to_third)
        up_gradient(kept, slope, second, third, rows_in, rows_out, grad_lin)
        wait_all(to_first)
        input_gradient(targets, result, kept, first)


def middle_gradient(cotangent, kept, fourth, rows_in, rows_out):
    blocks, rows, width = cotangent.shape
    kept[:, 0] = cotangent[...]
    for a, product in block_tiles(lambda a: cotangent[a], fourth):
        rows_in[pl.ds(a * rows, 2 * rows), :] = product
    exchange_blocks(rows_in, rows_out, blocks, rows)
    kept[:, 1] = rows_out[...].reshape(blocks, rows, width).astype(jnp.bfloat16)


def up_gradient(kept, slope, second, third, rows_in, rows_out, grad_lin):
    blocks, _, rows, width = kept.shape
    owned = third.shape[1]
    for b in range(blocks):
        grad_hid = jnp.dot(
            kept[b, 1], third[b // owned, b % owned], preferred_element_type=jnp.float32
        )
        grad_lin[b] = (grad_hid * slope[b]).astype(jnp.bfloat16)
    for b in range(blocks):
        rows_in[pl.ds(b * rows, rows), :] = jnp.dot(
            grad_lin[b], second[b // owned, b % owned], preferred_element_type=jnp.float32
        )
    exchange_blocks(rows_in, rows_out, blocks, rows)
    kept[:, 2] = rows_out[...].reshape(blocks, rows, width).astype(jnp.bfloat16)


def input_gradient(cotangent, result, kept, first):
    rows = cotangent.shape[1]
    for a, product in block_tiles(lambda a: kept[a, 2], first):
        for i in range(2):
            total = cotangent[a + i].astype(jnp.float32) + product[i * rows : (i + 1) * rows]
            result[a + i] = total.astype(jnp.bfloat16)


def step_body(
    turn, section, cotangent, old_kept, slope, second, fourth, third, first, *outputs_and_scratch
):
    *result, kept, rows_in, rows_out, grad_lin = outputs_and_scratch

    @pl.when(section[0] != turn)
    def _():
        kept[...] = old_kept[...]

    @pl.when(section[0] == turn)
    def _():
        middle_gradient(cotangent, kept, fourth, rows_in, rows_out)
        up_gradient(kept, slope, second, third, rows_in, rows_out, grad_lin)
        if result:
            input_gradient(cotangent, result[0], kept, first)


def reload_body(gathered, paired, second, fourth, third, first, sems):
    groups = loads_of(gathered, paired, second, fourth, third, first, sems)
    for copies in groups:
        start_all(copies)
    for copies in groups:
        wait_all(copies)


def gradients_body(
    returned,
    w1,
    w3,
    inputs,
    mixed,
    gelu_rows,
    slope,
    handed_back,
    grad_inputs,
    grad_w1,
    grad_w2,
    grad_w3,
    grad_w4,
):
    devices, owned, _, rows, width = returned.shape
    order = order_matrix(width, devices * owned, width // (devices * owned))

    def rows_of(block, kind):
        value = returned[:, block, kind].astype(jnp.float32)
        return value.reshape(devices * rows, width)

    def in_natural_order(value):
        return jnp.dot(
            value.astype(jnp.bfloat16), order, preferred_element_type=jnp.float32
        ).astype(jnp.bfloat16)

    for a in range(owned):
        gy = rows_of(a, 0)
        gu = in_natural_order(rows_of(a, 2))
        grad_inputs[:, a * width : (a + 1) * width] = (gy + contract_last(gu, w1[a])).astype(
            jnp.bfloat16
        )
        grad_w1[a] = jnp.dot(inputs[a], gu, preferred_element_type=jnp.float32)
        grad_w4[a] = jnp.dot(
            handed_back[a], gy.astype(jnp.bfloat16), preferred_element_type=jnp.float32
        )
    for b in range(owned):
        gv = in_natural_order(rows_of(b, 1))
        grad_lin = (contract_last(w3[b], gv) * slope[b]).astype(jnp.bfloat16)
        grad_w2[b] = contract_last(mixed[b], grad_lin)
        grad_w3[b] = jnp.dot(gelu_rows[b], gv, preferred_element_type=jnp.float32)


def in_vmem(count):
    return [IN_VMEM] * count


def to_owners(value):
    return lax.all_to_all(value, "tensor", split_axis=0, concat_axis=0, tiled=True)


def local(section_inputs, out_grad, w1, w2, w3, w4):
    devices = lax.axis_size("tensor")
    section_count = lax.axis_size("section")
    section = lax.axis_index("section").astype(jnp.int32).reshape(1)
    all_rows = section_inputs.shape[1] * section_inputs.shape[2]
    owned, width, hidden = w2.shape[1:]
    blocks = owned * devices
    spread = width // blocks
    rows = all_rows // devices
    packed_rows = owned * (2 * hidden + 2 * width)
    bf16, f32 = jnp.bfloat16, jnp.float32

    packed = pl.pallas_call(
        functools.partial(prepare_body, blocks),
        out_shape=jax.ShapeDtypeStruct((packed_rows, width), bf16),
        in_specs=[IN_HBM] * 4,
        out_specs=IN_VMEM,
        scratch_shapes=[pltpu.VMEM(w.shape[1:], bf16) for w in (w1, w2, w3, w4)]
        + [pltpu.SemaphoreType.DMA((4,))],
        compiler_params=pltpu.CompilerParams(vmem_limit_bytes=60 * MIB),
        name="prepare_weights",
    )(w1[0], w2[0], w3[0], w4[0])
    gathered = lax.all_gather(packed, "tensor", axis=0, tiled=False)

    input_rows = section_inputs[0].reshape(all_rows, owned, width)
    first_local = packed[packed_rows - owned * width :].reshape(owned, width, width)
    raised = matrix_product("tac,apc->atp", input_rows, first_local).astype(bf16)
    raised = raised.reshape(owned, devices, rows, width).transpose(1, 0, 2, 3)
    raised = to_owners(raised).reshape(blocks, rows, width)
    share = rows * owned // section_count
    targets = out_grad.reshape(devices, section_count, share, width)
    targets = lax.dynamic_index_in_dim(targets, section[0], axis=1, keepdims=False)
    targets = lax.all_gather(to_owners(targets), "section", axis=1, tiled=False)
    targets = targets.reshape(devices, rows, owned, width).transpose(0, 2, 1, 3)
    targets = targets.reshape(blocks, rows, width)

    def forward(input_rows, w1, w2, w3):
        raised_rows = matrix_product("owz,wzy->wyo", input_rows, w1).astype(bf16)
        mixed = lax.all_to_all(raised_rows, "tensor", split_axis=1, concat_axis=0, tiled=True)
        mixed = mixed.reshape(blocks, owned, spread, all_rows).transpose(1, 0, 2, 3)
        mixed = mixed.reshape(owned, width, all_rows)
        linear = matrix_product("bkt,bkn->bnt", mixed, w2)
        gelu_rows = gelu_tanh(linear).astype(bf16)
        slope = gelu_slope(linear)
        lowered = matrix_product("bnt,bnk->bkt", gelu_rows, w3).astype(bf16)
        back = lax.all_to_all(lowered, "tensor", split_axis=1, concat_axis=0, tiled=True)
        back = back.reshape(blocks, owned, spread, all_rows).transpose(1, 0, 2, 3)
        back = back.reshape(owned, width, all_rows)
        return input_rows.transpose(1, 2, 0), mixed, gelu_rows, slope, back

    weight_shapes = [
        pltpu.VMEM((devices, owned, hidden, width), bf16),
        pltpu.VMEM((devices // 2, owned * width, 2 * width), bf16),
        pltpu.VMEM((devices, owned, width, hidden), bf16),
        pltpu.VMEM((devices // 2, owned * width, 2 * width), bf16),
    ]
    copies = pltpu.SemaphoreType.DMA((owned * (5 + hidden // width),))
    row_shape = jax.ShapeDtypeStruct((blocks, rows, width), bf16)
    kept_shape = jax.ShapeDtypeStruct((blocks, 3, rows, width), bf16)
    scratch = [
        pltpu.VMEM((blocks * rows, width), f32),
        pltpu.VMEM((blocks * rows, width), f32),
        pltpu.VMEM((blocks, rows, hidden), bf16),
    ]
    last = section_count - 1
    gathered, raised, targets = lax.optimization_barrier((gathered, raised, targets))
    cotangent, kept, slope, *weights = pl.pallas_call(
        functools.partial(first_body, last),
        out_shape=[row_shape, kept_shape, pltpu.VMEM((blocks, rows, hidden), f32)]
        + weight_shapes,
        in_specs=[IN_SMEM, IN_VMEM, IN_VMEM, IN_HBM, IN_HBM],
        out_specs=in_vmem(7),
        scratch_shapes=scratch + [copies],
        compiler_params=pltpu.CompilerParams(vmem_limit_bytes=28 * MIB),
        name="load_and_first_section",
    )(section, raised, targets, gathered, gathered.reshape(devices // 2, 2, packed_rows, width))
    for turn in range(last, -1, -1):
        if turn < last:
            cotangent = lax.ppermute(cotangent, "section", [(turn + 1, turn)])
            out_shapes = [row_shape, kept_shape] if turn > 0 else [kept_shape]
            *cotangents, kept = pl.pallas_call(
                functools.partial(step_body, turn),
                out_shape=out_shapes,
                in_specs=[IN_SMEM] + in_vmem(7),
                out_specs=in_vmem(len(out_shapes)),
                scratch_shapes=scratch,
                compiler_params=pltpu.CompilerParams(vmem_limit_bytes=8 * MIB),
                name="section_step",
            )(section, cotangent, kept, slope, *weights)
            cotangent = cotangents[0] if turn > 0 else None
        if turn == section_count // 2:
            kept, given = lax.optimization_barrier((kept, (input_rows, w1[0], w2[0], w3[0])))
            nothing = jax.tree.map(
                lambda value: jnp.zeros(value.shape, value.dtype), jax.eval_shape(forward, *given)
            )
            forward_values = lax.cond(
                section[0] >= 0, lambda *given: forward(*given), lambda *given: nothing, *given
            )
            gathered, forward_values = lax.optimization_barrier((gathered, forward_values))
            weights = pl.pallas_call(
                reload_body,
                out_shape=weight_shapes,
                in_specs=[IN_HBM, IN_HBM],
                out_specs=in_vmem(4),
                scratch_shapes=[copies],
                compiler_params=pltpu.CompilerParams(vmem_limit_bytes=28 * MIB),
                name="load_again",
            )(gathered, gathered.reshape(devices // 2, 2, packed_rows, width))

    returned = to_owners(kept.reshape(devices, owned, 3, rows, width))
    grad_inputs, *grads = pl.pallas_call(
        gradients_body,
        out_shape=[
            jax.ShapeDtypeStruct((all_rows, owned * width), bf16),
            jax.ShapeDtypeStruct((owned, width, width), f32),
            jax.ShapeDtypeStruct((owned, width, hidden), f32),
            jax.ShapeDtypeStruct((owned, hidden, width), f32),
            jax.ShapeDtypeStruct((owned, width, width), f32),
        ],
        in_specs=in_vmem(8),
        out_specs=in_vmem(5),
        compiler_params=pltpu.CompilerParams(vmem_limit_bytes=24 * MIB),
        name="gradients",
    )(returned, w1[0], w3[0], *forward_values)
    grad_inputs = grad_inputs.reshape(section_inputs.shape)
    return (grad_inputs, *[grad[None] for grad in grads])


def solution(mesh):
    in_specs = (
        P("section", None, None, "tensor"),
        P(None, None, "tensor"),
        P("section", "tensor", None, None),
        P("section", "tensor", None, None),
        P("section", "tensor", None, None),
        P("section", "tensor", None, None),
    )
    out_specs = (
        P("section", None, None, "tensor"),
        P("section", "tensor", None, None),
        P("section", "tensor", None, None),
        P("section", "tensor", None, None),
        P("section", "tensor", None, None),
    )
    return jax.shard_map(local, mesh=mesh, in_specs=in_specs, out_specs=out_specs, check_vma=False)
```

```python
import functools

import jax
import jax.numpy as jnp
from jax import lax
from jax.experimental import pallas as pl
from jax.experimental.pallas import tpu as pltpu
from jax.sharding import PartitionSpec as P

SQRT_TWO_PI = 0.7978845608028654
CUBIC_TERM = 0.044715
MIB = 2**20

IN_VMEM = pl.BlockSpec(memory_space=pltpu.VMEM)
IN_SMEM = pl.BlockSpec(memory_space=pltpu.SMEM)
IN_HBM = pl.BlockSpec(memory_space=pltpu.HBM)


def gelu_tanh(linear):
    inner = SQRT_TWO_PI * (linear + CUBIC_TERM * linear * linear * linear)
    return 0.5 * linear * (1.0 + jnp.tanh(inner))


def gelu_slope(linear):
    inner = SQRT_TWO_PI * (linear + CUBIC_TERM * linear * linear * linear)
    tangent = jnp.tanh(inner)
    return 0.5 * (1.0 + tangent) + 0.5 * linear * (1.0 - tangent * tangent) * SQRT_TWO_PI * (
        1.0 + 3.0 * CUBIC_TERM * linear * linear
    )


def matrix_product(form, left_side, right_side):
    return jnp.einsum(form, left_side, right_side, preferred_element_type=jnp.float32)


def exchange_blocks(source, target, blocks, rows):
    for row in range(0, rows, 2):
        pair = [source[pl.ds(row + i, blocks, stride=rows), :] for i in range(2)]
        turned = jnp.concatenate(pair, axis=0).T
        for i in range(2):
            lanes = slice(i * blocks, (i + 1) * blocks)
            target[pl.ds(row + i, blocks, stride=rows), :] = jnp.concatenate(
                [turned[:blocks, lanes], turned[blocks:, lanes]], axis=1
            )


def contract_last(left_side, right_side):
    return lax.dot_general(
        left_side, right_side, (((1,), (1,)), ((), ())), preferred_element_type=jnp.float32
    )


def order_matrix(width, blocks, spread):
    grouped = lax.broadcasted_iota(jnp.int32, (width, width), 0)
    natural = lax.broadcasted_iota(jnp.int32, (width, width), 1)
    here = grouped == (natural % spread) * blocks + natural // spread
    return jnp.where(here, 1.0, 0.0).astype(jnp.bfloat16)


def prepare_body(blocks, w1_far, w2_far, w3_far, w4_far, packed, w1, w2, w3, w4, sems):
    owned, width, hidden = w2.shape
    pairs = ((w2_far, w2), (w4_far, w4), (w3_far, w3), (w1_far, w1))
    copies = [pltpu.make_async_copy(*pair, sems.at[i]) for i, pair in enumerate(pairs)]
    for copy in copies:
        copy.start()
    order = order_matrix(width, blocks, width // blocks)
    for copy in copies:
        copy.wait()
    base = 0
    for b in range(owned):
        turned = jnp.dot(order, w2[b], preferred_element_type=jnp.float32).T
        packed[pl.ds(base, hidden), :] = turned.astype(jnp.bfloat16)
        base += hidden
    for a in range(owned):
        turned = jnp.dot(order, w4[a], preferred_element_type=jnp.float32).T
        packed[pl.ds(base, width), :] = turned.astype(jnp.bfloat16)
        base += width
    for b in range(owned):
        for part in range(hidden // width):
            piece = contract_last(order, w3[b, pl.ds(part * width, width), :])
            packed[pl.ds(base, width), :] = piece.astype(jnp.bfloat16)
            base += width
    for a in range(owned):
        packed[pl.ds(base, width), :] = contract_last(order, w1[a]).astype(jnp.bfloat16)
        base += width


def loads_of(gathered, paired, second, fourth, third, first, sems):
    owned, width, hidden = third.shape[1:]
    to_second, to_fourth, to_third, to_first = [], [], [], []
    base = 0
    for half in range(owned):
        to_second.append((gathered.at[:, pl.ds(base, hidden), :], second.at[:, half]))
        base += hidden
    for target, group, start in (
        (fourth, to_fourth, base),
        (first, to_first, base + owned * (width + hidden)),
    ):
        for half in range(owned):
            for side in range(2):
                piece = paired.at[:, side, pl.ds(start + half * width, width), :]
                place = target.at[:, pl.ds(half * width, width), pl.ds(side * width, width)]
                group.append((piece, place))
    base += owned * width
    for half in range(owned):
        for part in range(hidden // width):
            place = third.at[:, half, :, pl.ds(part * width, width)]
            to_third.append((gathered.at[:, pl.ds(base, width), :], place))
            base += width
    groups, number = [], 0
    for group in (to_second, to_fourth, to_third, to_first):
        copies = []
        for source, target in group:
            copies.append(pltpu.make_async_copy(source, target, sems.at[number]))
            number += 1
        groups.append(copies)
    return groups


def start_all(copies):
    for copy in copies:
        copy.start()


def block_tiles(rows_of, tiles):
    for number in range(tiles.shape[0]):
        four = [rows_of(4 * number + i) for i in range(4)]
        empty = jnp.zeros_like(four[0])
        spread = [
            jnp.concatenate([value, empty] if i % 2 == 0 else [empty, value], axis=1)
            for i, value in enumerate(four)
        ]
        product = jnp.dot(
            jnp.concatenate(spread, axis=0), tiles[number], preferred_element_type=jnp.float32
        )
        pair = 2 * four[0].shape[0]
        width = four[0].shape[1]
        yield 4 * number, product[:pair, :width]
        yield 4 * number + 2, product[pair:, width:]


def wait_all(copies):
    for copy in copies:
        copy.wait()


def first_body(
    turn,
    section,
    raised,
    targets,
    gathered,
    paired,
    result,
    kept,
    slope,
    second,
    fourth,
    third,
    first,
    rows_in,
    rows_out,
    grad_lin,
    sems,
):
    blocks, rows, width = raised.shape
    owned = third.shape[1]
    to_second, to_fourth, to_third, to_first = loads_of(
        gathered, paired, second, fourth, third, first, sems
    )
    start_all(to_fourth + to_second)

    @pl.when(section[0] == turn)
    def _():
        wait_all(to_fourth)
        middle_gradient(targets, kept, fourth, rows_in, rows_out)

    rows_in[...] = raised[...].astype(jnp.float32).reshape(blocks * rows, width)
    exchange_blocks(rows_in, rows_out, blocks, rows)
    start_all(to_third + to_first)
    halves = [list(range(half, blocks, owned)) for half in range(owned)]
    for b in sum(halves, []):
        if b < owned:
            to_second[b].wait()
        mixed = rows_out[pl.ds(b * rows, rows), :].astype(jnp.bfloat16)
        slope[b] = gelu_slope(contract_last(mixed, second[b // owned, b % owned]))

    @pl.when(section[0] != turn)
    def _():
        wait_all(to_fourth + to_third + to_first)

    @pl.when(section[0] == turn)
    def _():
        up_gradient(kept, slope, second, third, rows_in, rows_out, grad_lin, to_third)
        wait_all(to_first)
        input_gradient(targets, result, kept, first)


def middle_gradient(cotangent, kept, fourth, rows_in, rows_out):
    blocks, rows, width = cotangent.shape
    kept[:, 0] = cotangent[...]
    for a, product in block_tiles(lambda a: cotangent[a], fourth):
        rows_in[pl.ds(a * rows, 2 * rows), :] = product
    exchange_blocks(rows_in, rows_out, blocks, rows)
    kept[:, 1] = rows_out[...].reshape(blocks, rows, width).astype(jnp.bfloat16)


def up_gradient(kept, slope, second, third, rows_in, rows_out, grad_lin, loads=()):
    blocks, _, rows, width = kept.shape
    owned = third.shape[1]
    halves = [list(range(half, blocks, owned)) for half in range(owned)]
    per_half = len(loads) // owned
    for b in sum(halves, []):
        if b < owned:
            wait_all(loads[b * per_half : (b + 1) * per_half])
        grad_hid = jnp.dot(
            kept[b, 1], third[b // owned, b % owned], preferred_element_type=jnp.float32
        )
        grad_lin[b] = (grad_hid * slope[b]).astype(jnp.bfloat16)
    for b in range(blocks):
        rows_in[pl.ds(b * rows, rows), :] = jnp.dot(
            grad_lin[b], second[b // owned, b % owned], preferred_element_type=jnp.float32
        )
    exchange_blocks(rows_in, rows_out, blocks, rows)
    kept[:, 2] = rows_out[...].reshape(blocks, rows, width).astype(jnp.bfloat16)


def input_gradient(cotangent, result, kept, first):
    rows = cotangent.shape[1]
    for a, product in block_tiles(lambda a: kept[a, 2], first):
        for i in range(2):
            total = cotangent[a + i].astype(jnp.float32) + product[i * rows : (i + 1) * rows]
            result[a + i] = total.astype(jnp.bfloat16)


def step_body(
    turn, section, cotangent, old_kept, slope, second, fourth, third, first, *outputs_and_scratch
):
    *result, kept, rows_in, rows_out, grad_lin = outputs_and_scratch

    @pl.when(section[0] != turn)
    def _():
        kept[...] = old_kept[...]

    @pl.when(section[0] == turn)
    def _():
        middle_gradient(cotangent, kept, fourth, rows_in, rows_out)
        up_gradient(kept, slope, second, third, rows_in, rows_out, grad_lin)
        if result:
            input_gradient(cotangent, result[0], kept, first)


def reload_body(gathered, paired, second, fourth, third, first, sems):
    groups = loads_of(gathered, paired, second, fourth, third, first, sems)
    for copies in groups:
        start_all(copies)
    for copies in groups:
        wait_all(copies)


def gradients_body(
    returned,
    w1,
    w3,
    inputs,
    mixed,
    gelu_rows,
    slope,
    handed_back,
    grad_inputs,
    grad_w1,
    grad_w2,
    grad_w3,
    grad_w4,
):
    devices, owned, _, rows, width = returned.shape
    order = order_matrix(width, devices * owned, width // (devices * owned))

    def rows_of(block, kind):
        value = returned[:, block, kind].astype(jnp.float32)
        return value.reshape(devices * rows, width)

    def in_natural_order(value):
        return jnp.dot(
            value.astype(jnp.bfloat16), order, preferred_element_type=jnp.float32
        ).astype(jnp.bfloat16)

    for a in range(owned):
        gy = rows_of(a, 0)
        gu = in_natural_order(rows_of(a, 2))
        grad_inputs[:, a * width : (a + 1) * width] = (gy + contract_last(gu, w1[a])).astype(
            jnp.bfloat16
        )
        grad_w1[a] = jnp.dot(inputs[a], gu, preferred_element_type=jnp.float32)
        grad_w4[a] = jnp.dot(
            handed_back[a], gy.astype(jnp.bfloat16), preferred_element_type=jnp.float32
        )
    for b in range(owned):
        gv = in_natural_order(rows_of(b, 1))
        grad_lin = (contract_last(w3[b], gv) * slope[b]).astype(jnp.bfloat16)
        grad_w2[b] = contract_last(mixed[b], grad_lin)
        grad_w3[b] = jnp.dot(gelu_rows[b], gv, preferred_element_type=jnp.float32)


def in_vmem(count):
    return [IN_VMEM] * count


def to_owners(value):
    return lax.all_to_all(value, "tensor", split_axis=0, concat_axis=0, tiled=True)


def local(section_inputs, out_grad, w1, w2, w3, w4):
    devices = lax.axis_size("tensor")
    section_count = lax.axis_size("section")
    section = lax.axis_index("section").astype(jnp.int32).reshape(1)
    all_rows = section_inputs.shape[1] * section_inputs.shape[2]
    owned, width, hidden = w2.shape[1:]
    blocks = owned * devices
    spread = width // blocks
    rows = all_rows // devices
    packed_rows = owned * (2 * hidden + 2 * width)
    bf16, f32 = jnp.bfloat16, jnp.float32

    packed = pl.pallas_call(
        functools.partial(prepare_body, blocks),
        out_shape=jax.ShapeDtypeStruct((packed_rows, width), bf16),
        in_specs=[IN_HBM] * 4,
        out_specs=IN_VMEM,
        scratch_shapes=[pltpu.VMEM(w.shape[1:], bf16) for w in (w1, w2, w3, w4)]
        + [pltpu.SemaphoreType.DMA((4,))],
        compiler_params=pltpu.CompilerParams(vmem_limit_bytes=60 * MIB),
        name="prepare_weights",
    )(w1[0], w2[0], w3[0], w4[0])
    gathered = lax.all_gather(packed, "tensor", axis=0, tiled=False)

    input_rows = section_inputs[0].reshape(all_rows, owned, width)
    first_local = packed[packed_rows - owned * width :].reshape(owned, width, width)
    raised = matrix_product("tac,apc->atp", input_rows, first_local).astype(bf16)
    raised = raised.reshape(owned, devices, rows, width).transpose(1, 0, 2, 3)
    raised = to_owners(raised).reshape(blocks, rows, width)
    share = rows * owned // section_count
    targets = out_grad.reshape(devices, section_count, share, width)
    targets = lax.dynamic_index_in_dim(targets, section[0], axis=1, keepdims=False)
    targets = lax.all_gather(to_owners(targets), "section", axis=1, tiled=False)
    targets = targets.reshape(devices, rows, owned, width).transpose(0, 2, 1, 3)
    targets = targets.reshape(blocks, rows, width)

    def forward(input_rows, w1, w2, w3):
        raised_rows = matrix_product("owz,wzy->wyo", input_rows, w1).astype(bf16)
        mixed = lax.all_to_all(raised_rows, "tensor", split_axis=1, concat_axis=0, tiled=True)
        mixed = mixed.reshape(blocks, owned, spread, all_rows).transpose(1, 0, 2, 3)
        mixed = mixed.reshape(owned, width, all_rows)
        linear = matrix_product("bkt,bkn->bnt", mixed, w2)
        gelu_rows = gelu_tanh(linear).astype(bf16)
        slope = gelu_slope(linear)
        lowered = matrix_product("bnt,bnk->bkt", gelu_rows, w3).astype(bf16)
        back = lax.all_to_all(lowered, "tensor", split_axis=1, concat_axis=0, tiled=True)
        back = back.reshape(blocks, owned, spread, all_rows).transpose(1, 0, 2, 3)
        back = back.reshape(owned, width, all_rows)
        return input_rows.transpose(1, 2, 0), mixed, gelu_rows, slope, back

    weight_shapes = [
        pltpu.VMEM((devices, owned, hidden, width), bf16),
        pltpu.VMEM((devices // 2, owned * width, 2 * width), bf16),
        pltpu.VMEM((devices, owned, width, hidden), bf16),
        pltpu.VMEM((devices // 2, owned * width, 2 * width), bf16),
    ]
    copies = pltpu.SemaphoreType.DMA((owned * (5 + hidden // width),))
    row_shape = jax.ShapeDtypeStruct((blocks, rows, width), bf16)
    kept_shape = jax.ShapeDtypeStruct((blocks, 3, rows, width), bf16)
    scratch = [
        pltpu.VMEM((blocks * rows, width), f32),
        pltpu.VMEM((blocks * rows, width), f32),
        pltpu.VMEM((blocks, rows, hidden), bf16),
    ]
    last = section_count - 1
    gathered, raised, targets = lax.optimization_barrier((gathered, raised, targets))
    cotangent, kept, slope, *weights = pl.pallas_call(
        functools.partial(first_body, last),
        out_shape=[row_shape, kept_shape, pltpu.VMEM((blocks, rows, hidden), f32)]
        + weight_shapes,
        in_specs=[IN_SMEM, IN_VMEM, IN_VMEM, IN_HBM, IN_HBM],
        out_specs=in_vmem(7),
        scratch_shapes=scratch + [copies],
        compiler_params=pltpu.CompilerParams(vmem_limit_bytes=28 * MIB),
        name="load_and_first_section",
    )(section, raised, targets, gathered, gathered.reshape(devices // 2, 2, packed_rows, width))
    for turn in range(last, -1, -1):
        if turn < last:
            cotangent = lax.ppermute(cotangent, "section", [(turn + 1, turn)])
            out_shapes = [row_shape, kept_shape] if turn > 0 else [kept_shape]
            *cotangents, kept = pl.pallas_call(
                functools.partial(step_body, turn),
                out_shape=out_shapes,
                in_specs=[IN_SMEM] + in_vmem(7),
                out_specs=in_vmem(len(out_shapes)),
                scratch_shapes=scratch,
                compiler_params=pltpu.CompilerParams(vmem_limit_bytes=8 * MIB),
                name="section_step",
            )(section, cotangent, kept, slope, *weights)
            cotangent = cotangents[0] if turn > 0 else None
        if turn == section_count // 2:
            kept, given = lax.optimization_barrier((kept, (input_rows, w1[0], w2[0], w3[0])))
            nothing = jax.tree.map(
                lambda value: jnp.zeros(value.shape, value.dtype), jax.eval_shape(forward, *given)
            )
            forward_values = lax.cond(
                section[0] >= 0, lambda *given: forward(*given), lambda *given: nothing, *given
            )
            gathered, forward_values = lax.optimization_barrier((gathered, forward_values))
            weights = pl.pallas_call(
                reload_body,
                out_shape=weight_shapes,
                in_specs=[IN_HBM, IN_HBM],
                out_specs=in_vmem(4),
                scratch_shapes=[copies],
                compiler_params=pltpu.CompilerParams(vmem_limit_bytes=28 * MIB),
                name="load_again",
            )(gathered, gathered.reshape(devices // 2, 2, packed_rows, width))

    returned = to_owners(kept.reshape(devices, owned, 3, rows, width))
    grad_inputs, *grads = pl.pallas_call(
        gradients_body,
        out_shape=[
            jax.ShapeDtypeStruct((all_rows, owned * width), bf16),
            jax.ShapeDtypeStruct((owned, width, width), f32),
            jax.ShapeDtypeStruct((owned, width, hidden), f32),
            jax.ShapeDtypeStruct((owned, hidden, width), f32),
            jax.ShapeDtypeStruct((owned, width, width), f32),
        ],
        in_specs=in_vmem(8),
        out_specs=in_vmem(5),
        compiler_params=pltpu.CompilerParams(vmem_limit_bytes=24 * MIB),
        name="gradients",
    )(returned, w1[0], w3[0], *forward_values)
    grad_inputs = grad_inputs.reshape(section_inputs.shape)
    return (grad_inputs, *[grad[None] for grad in grads])


def solution(mesh):
    in_specs = (
        P("section", None, None, "tensor"),
        P(None, None, "tensor"),
        P("section", "tensor", None, None),
        P("section", "tensor", None, None),
        P("section", "tensor", None, None),
        P("section", "tensor", None, None),
    )
    out_specs = (
        P("section", None, None, "tensor"),
        P("section", "tensor", None, None),
        P("section", "tensor", None, None),
        P("section", "tensor", None, None),
        P("section", "tensor", None, None),
    )
    return jax.shard_map(local, mesh=mesh, in_specs=in_specs, out_specs=out_specs, check_vma=False)
```
